256 devices in a mesh: row: 16 (over x, y), col: 16 (over z, core).
Axes of the slice: x: 4, y: 4, z: 8, core: 2. Of those that a mesh axis runs over, the one named last changes fastest.
Arguments:
- layer_input: bfloat16 [2048, 8192], P('col', 'row'), may hold values from -6 to 6
- output_grad: bfloat16 [2048, 8192], P('col', 'row'), may hold values from -0.59765625 to 0.59765625
- inproj_weight: bfloat16 [8192, 16384], P('row', 'col'), may hold values from -0.0625 to 0.0625
- outproj_weight: bfloat16 [16384, 8192], P('col', 'row'), may hold values from -0.046875 to 0.046875
- input_coeffs: bfloat16 [2048, 2048], P('row'), may hold values from -6 to 6
- output_coeffs: bfloat16 [2048, 2048], P('row'), may hold values from -0.059814453 to 0.059814453
- step_sizes: float32 [256, 2048], P('col', 'row'), may hold values from 0.2 to 1
- log_decay: float32 [256, 2048], P('col', 'row'), may hold values from -1 to 0
- state_start: float32 [256, 64, 256], P('col'), may hold values from -60 to 60
- state_grad: float32 [256, 64, 256], P('col'), may hold values from -0.3 to 0.3
Outputs:
- input_grad: bfloat16 [2048, 8192], P('col', 'row')
- inproj_grad: float32 [8192, 16384], P('row', 'col')
- outproj_grad: float32 [16384, 8192], P('col', 'row')
- incoeff_grad: float32 [2048, 2048], P('row', 'col')
- outcoeff_grad: float32 [2048, 2048], P('row', 'col')
- steps_grad: float32 [256, 2048], P('col', 'row')
- decay_grad: float32 [256, 2048], P('col', 'row')
The draws below stay inside these ranges and needn't reach their ends.
All inputs are finite; a program needn't handle non-finite values.
Results may differ from the reference program's by a relative error of at most 0.04.
Values may be sent and summed in bfloat16 or wider, within the bound.
No kernel may reach another device: no remote copies, remote signals or barrier semaphores. Data moves between devices by JAX's collectives and lax.ppermute only.
A program may use at most 128 MiB of HBM per device.

```python
import math
import jax
import jax.numpy as jnp
from jax import lax

D = 8192
HEADS = 256
HEAD_DIM = 64
STATE = 256
SPAN = 128
TOK_DEV = 128
WINDOW_TOKENS = 2048
INNER = 16384
GROUPS = 8
N_ROW = 16
N_COL = 16


def draw_log_decay(key, part):
    key = jax.random.fold_in(key, 7)
    random_subkeys = jax.random.split(key, 7)
    fast_share = 0.5
    fast_heads = jax.random.uniform(random_subkeys[0], (HEADS,), jnp.float32) < fast_share
    fast_rate = jnp.exp(jax.random.uniform(random_subkeys[1], (HEADS,), jnp.float32, math.log(1.0 / 50.0), math.log(1.0 / 30.0)))
    slow_rate = jax.random.uniform(random_subkeys[2], (HEADS,), jnp.float32, 0.3, 0.6) / WINDOW_TOKENS
    head_decay_rate = jnp.where(fast_heads, fast_rate, slow_rate)
    block_count = WINDOW_TOKENS // TOK_DEV
    block_multiplier = jnp.exp(jax.random.uniform(random_subkeys[3], (HEADS, block_count), jnp.float32, math.log(0.5), math.log(2.0)))
    block_multiplier = jnp.repeat(block_multiplier, TOK_DEV, axis=1)
    position_multiplier = jax.random.uniform(random_subkeys[4], (HEADS, WINDOW_TOKENS), jnp.float32, 0.5, 1.5)
    token_group_start = jax.random.randint(random_subkeys[5], (2,), 0, WINDOW_TOKENS)
    token_group_length = jax.random.uniform(random_subkeys[6], (2,), jnp.float32, 0.25, 0.7)
    token_positions = jnp.arange(WINDOW_TOKENS)
    token_group = jnp.sum(jnp.where(token_positions[None, :] == token_group_start[:, None], token_group_length[:, None], 0.0), axis=0)
    return -(head_decay_rate[:, None] * block_multiplier * position_multiplier) - token_group[None, :]


def block_levels(key, extent, shards, least, top_value):
    level = 1.0
    for dim, shards_of in shards:
        steps = jax.random.uniform(jax.random.fold_in(jax.random.fold_in(key, 6), dim), (shards_of,), jnp.float32, least / len(shards), top_value / len(shards))
        level = level * jnp.repeat(jnp.exp(steps), extent[dim] // shards_of).reshape((-1,) + (1,) * (len(extent) - 1 - dim))
    return level


def centred(stream_key, dims, scale, reach, shards=(), kind=jnp.bfloat16):
    drawn = jax.random.normal(stream_key, dims, jnp.float32) * scale
    if len(shards) > 0:
        drawn = block_levels(stream_key, dims, shards, -0.22, 0.18) * drawn
    return jnp.clip(drawn, min=-reach, max=reach).astype(kind)


def setup_inputs(seed: int = 0) -> dict:
    keys = jax.random.split(jax.random.key(seed), 11)
    return {
        "layer_input": centred(keys[0], (WINDOW_TOKENS, D), 1.0, 6.0, ((0, 16), (1, 16))),
        "output_grad": centred(keys[1], (WINDOW_TOKENS, D), 0.1, 0.59765625, ((0, 16), (1, 16))),
        "inproj_weight": centred(keys[2], (D, INNER), D ** -0.5, 0.0625, ((0, 16), (1, 16))),
        "outproj_weight": centred(keys[3], (INNER, D), INNER ** -0.5, 0.046875, ((0, 16), (1, 16))),
        "input_coeffs": centred(keys[4], (WINDOW_TOKENS, GROUPS * STATE), 1.0, 6.0, ((0, 16),)),
        "output_coeffs": centred(keys[5], (WINDOW_TOKENS, GROUPS * STATE), 0.01, 0.059814453, ((0, 16),)),
        "step_sizes": jnp.clip(jnp.exp(math.log(1.0) - 1.609438 * jax.random.uniform(keys[6], (HEADS, WINDOW_TOKENS), jnp.float32) ** block_levels(keys[6], (HEADS, WINDOW_TOKENS), ((0, 16), (1, 16)), -0.2, 0.2)), 0.2, 1.0),
        "log_decay": draw_log_decay(jax.random.fold_in(keys[10], 71), 0),
        "state_start": centred(keys[8], (HEADS, HEAD_DIM, STATE), 10.0, 60.0, ((0, 16),), jnp.float32),
        "state_grad": centred(keys[9], (HEADS, HEAD_DIM, STATE), 0.05, 0.3, ((0, 16),), jnp.float32),
    }


precise = lax.Precision.HIGHEST

def round_trip(values):
    return lax.optimization_barrier(values.astype(jnp.bfloat16)).astype(jnp.float32)

def silu_slope(values):
    sigmoid_value = jax.nn.sigmoid(values)
    return sigmoid_value * (1.0 + values * (1.0 - sigmoid_value))

def span_forward(values, in_coeffs, out_coeffs, steps_in, decays, start_state):
    length = decays.shape[1]
    running = jnp.cumsum(decays, axis=1)
    lower = jnp.tril(jnp.ones((length, length), bool))[None]
    spread = running[:, :, None] - running[:, None, :]
    kernel = jnp.where(lower, jnp.exp(jnp.where(lower, spread, 0.0)), 0.0)
    scores = jnp.einsum('htn,hsn->hts', out_coeffs, in_coeffs, precision=precise)
    mixing = scores * kernel * steps_in[:, None, :]
    outputs = jnp.einsum('hts,hsp->htp', mixing, values, precision=precise)
    carried_in = jnp.einsum('htn,hpn->htp', out_coeffs, start_state, precision=precise)
    outputs = outputs + jnp.exp(running)[:, :, None] * carried_in
    closing = running[:, -1]
    carried = jnp.exp(closing[:, None] - running) * steps_in
    end_state = jnp.exp(closing)[:, None, None] * start_state
    end_state = end_state + jnp.einsum('hsp,hsn->hpn', values * carried[:, :, None], in_coeffs, precision=precise)
    return (outputs, end_state)

def split_spans(array, length):
    head_total = array.shape[0]
    shaped = array.reshape((head_total, array.shape[1] // length, length) + array.shape[2:])
    return jnp.moveaxis(shaped, 1, 0)

def join_spans(array):
    moved = jnp.moveaxis(array, 0, 1)
    return moved.reshape((moved.shape[0], moved.shape[1] * moved.shape[2]) + moved.shape[3:])

def run_forward(values, in_coeffs, out_coeffs, steps_in, decays, start_state, length):
    pieces = tuple((split_spans(item, length) for item in (values, in_coeffs, out_coeffs, steps_in, decays)))

    def advance(state, block_items):
        outputs, end_state = span_forward(*block_items, state)
        return (end_state, (outputs, state))
    end_state, stacked = lax.scan(advance, start_state, pieces)
    return (join_spans(stacked[0]), stacked[1], end_state)

def reference(layer_input, output_grad, inproj_weight, outproj_weight, input_coeffs, output_coeffs, step_sizes, log_decay, state_start, state_grad):
    width_block = D // N_ROW
    inner_block = INNER // N_COL
    preact = jnp.zeros((WINDOW_TOKENS, INNER), jnp.float32)
    mixed = jnp.zeros((WINDOW_TOKENS, INNER), jnp.float32)
    for block_index in range(N_ROW):
        lower_edge = block_index * width_block
        upper_edge = lower_edge + width_block
        preact = preact + round_trip(jnp.dot(layer_input[:, lower_edge:upper_edge], inproj_weight[lower_edge:upper_edge], preferred_element_type=jnp.float32))
        mixed = mixed + round_trip(jnp.dot(output_grad[:, lower_edge:upper_edge], outproj_weight[:, lower_edge:upper_edge].T, preferred_element_type=jnp.float32))
    mixed_grad = mixed.astype(jnp.bfloat16)
    signal = jax.nn.silu(preact).astype(jnp.bfloat16)
    values = signal.astype(jnp.float32).reshape(WINDOW_TOKENS, HEADS, HEAD_DIM).transpose(1, 0, 2)
    per_group = HEADS // GROUPS

    def expand(coeffs):
        grouped = coeffs.astype(jnp.float32).reshape(WINDOW_TOKENS, GROUPS, STATE).transpose(1, 0, 2)
        return jnp.repeat(grouped, per_group, axis=0)

    def whole_scan(values_in, in_heads, out_heads, steps_in, decays):
        outputs, starts, end_state = run_forward(values_in, in_heads, out_heads, steps_in, decays, state_start, SPAN)
        return (outputs, end_state)
    results, pullback = jax.vjp(whole_scan, values, expand(input_coeffs), expand(output_coeffs), step_sizes, log_decay)
    out_grads = mixed_grad.astype(jnp.float32).reshape(WINDOW_TOKENS, HEADS, HEAD_DIM).transpose(1, 0, 2)
    grads = pullback((out_grads, state_grad))
    scan_output = results[0].transpose(1, 0, 2).reshape(WINDOW_TOKENS, INNER).astype(jnp.bfloat16)
    signal_grad = grads[0].transpose(1, 0, 2).reshape(WINDOW_TOKENS, INNER)
    pre_grad = (signal_grad * silu_slope(preact)).astype(jnp.bfloat16)
    outproj_grad = jnp.dot(scan_output.T, output_grad, preferred_element_type=jnp.float32)
    inproj_grad = jnp.dot(layer_input.T, pre_grad, preferred_element_type=jnp.float32)
    layer_sum = jnp.zeros((WINDOW_TOKENS, D), jnp.float32)
    for block_index in range(N_COL):
        lower_edge = block_index * inner_block
        upper_edge = lower_edge + inner_block
        layer_sum = layer_sum + round_trip(jnp.dot(pre_grad[:, lower_edge:upper_edge], inproj_weight[:, lower_edge:upper_edge].T, preferred_element_type=jnp.float32))
    input_grad = layer_sum.astype(jnp.bfloat16)

    def collapse(grad_heads):
        summed = grad_heads.reshape(GROUPS, per_group, WINDOW_TOKENS, STATE).sum(axis=1)
        return summed.transpose(1, 0, 2).reshape(WINDOW_TOKENS, GROUPS * STATE)
    return (input_grad, inproj_grad, outproj_grad, collapse(grads[1]), collapse(grads[2]), grads[3], grads[4])
```

```python
import functools

import jax
import jax.numpy as jnp
from jax import lax
from jax.experimental import pallas as pl
from jax.experimental.pallas import tpu as pltpu
from jax.sharding import PartitionSpec as P

HEAD_DIM = 64
STATE = 256
SIDE = 4
DEPTH = 8
BLOCK = 128
CHUNK = 256
F32 = jnp.float32
BF16 = jnp.bfloat16


def shift_y(a, d):
    pairs = [(x * 4 + y, x * 4 + (y + d) % 4) for x in range(4) for y in range(4)]
    return lax.ppermute(a, "row", pairs)


def shift_x(a, d):
    pairs = [(x * 4 + y, (x + d) % 4 * 4 + y) for x in range(4) for y in range(4)]
    return lax.ppermute(a, "row", pairs)


def shift_z(a, d):
    pairs = [(z * 2 + c, (z + d) % 8 * 2 + c) for z in range(8) for c in range(2)]
    return lax.ppermute(a, "col", pairs)


def swap_core(a):
    return lax.ppermute(a, "col", [(i, i ^ 1) for i in range(16)])


def add(*terms):
    total = terms[0].astype(F32)
    for term in terms[1:]:
        total = total + term.astype(F32)
    return total


def gather_z(own):
    half = own.shape[0] // 2
    up1, down1 = shift_z(own, 1), shift_z(own, -1)
    up2, down2 = shift_z(up1, 1), shift_z(down1, -1)
    up3, down3 = shift_z(up2, 1), shift_z(down2, -1)
    far = (shift_z(up3[:half], 1), shift_z(down3[half:], -1))
    return jnp.concatenate([own, down1, down2, down3, *far, up3, up2, up1], axis=0)


def reduce_ring(chunks, shift):
    (c0a, c0b), (c1a, c1b), (c2a, c2b), (c3a, c3b) = chunks
    far_a, far_b = shift(c2a, 1), shift(c2b, -1)
    r1b, r3a = shift(c1b, 1), shift(c3a, -1)
    r1a = shift(add(c1a, far_a).astype(BF16), 1)
    r3b = shift(add(c3b, far_b).astype(BF16), -1)
    return (c0a, r1a, r3a), (c0b, r1b, r3b)


def reduce_grid(weights, tokens, first, second):
    chunks = []
    for d in range(SIDE):
        part = lax.dot_general(
            weights[d], tokens, (((1,), (1,)), ((), ())), preferred_element_type=F32
        ).astype(BF16)
        part = part.reshape(SIDE, HEAD_DIM, tokens.shape[0])
        chunks.append((part[:2], part[2:]))
    sums_a, sums_b = reduce_ring(chunks, first)
    near = add(*sums_a).astype(BF16)
    away = add(*sums_b).astype(BF16)
    half = HEAD_DIM // 2
    chunks = [(c[:half], c[half:]) for c in (near[0], near[1], away[0], away[1])]
    return reduce_ring(chunks, second)


def gather_ring(halves, shift):
    a, b = halves
    up_a, down_b = shift(a, 1), shift(b, -1)
    up_b, down_a = shift(b, 1), shift(a, -1)
    far_a, far_b = shift(up_a, 1), shift(down_b, -1)
    return [(a, b), (down_a, down_b), (far_a, far_b), (up_a, up_b)]


def gather_grid(own, first, second, first_at, second_at, first_axis):
    tokens = own.shape[1]
    half = HEAD_DIM // 2
    line = jnp.zeros((SIDE, HEAD_DIM, tokens), own.dtype)
    for d, pair in enumerate(gather_ring((own[:half], own[half:]), first)):
        at = (first_at + d) % SIDE
        for h, piece in enumerate(pair):
            line = lax.dynamic_update_slice(line, piece[None], (at, h * half, 0))
    whole = jnp.zeros((SIDE, SIDE, HEAD_DIM, tokens), own.dtype)
    for d, pair in enumerate(gather_ring((line[:2], line[2:]), second)):
        at = (second_at + d) % SIDE
        for h, piece in enumerate(pair):
            if first_axis == 1:
                whole = lax.dynamic_update_slice(whole, piece[None], (at, h * 2, 0, 0))
            else:
                whole = lax.dynamic_update_slice(whole, piece[:, None], (h * 2, at, 0, 0))
    return whole


def scatter_z(chunks):
    half = chunks[0].shape[0] // 2
    up = shift_z(chunks[4][:half].astype(BF16), 1)
    down = shift_z(chunks[4][half:].astype(BF16), -1)
    up_sum = jnp.concatenate([chunks[3][:half] + up.astype(F32), chunks[3][half:]], axis=0)
    down_sum = jnp.concatenate([chunks[5][:half], chunks[5][half:] + down.astype(F32)], axis=0)
    up, down = shift_z(up_sum.astype(BF16), 1), shift_z(down_sum.astype(BF16), -1)
    up = shift_z(add(chunks[2], up).astype(BF16), 1)
    down = shift_z(add(chunks[6], down).astype(BF16), -1)
    up = shift_z(add(chunks[1], up).astype(BF16), 1)
    down = shift_z(add(chunks[7], down).astype(BF16), -1)
    return add(chunks[0], up, down)


def dot(a, b, dims=((1,), (0,)), precision=None):
    return lax.dot_general(a, b, (dims, ((), ())), preferred_element_type=F32, precision=precision)


NT = ((1,), (1,))
TN = ((0,), (0,))
HIGH = lax.Precision.HIGHEST


def scan_kernel(place, *refs):
    sums = refs[:20]
    b_ref, c_ref, dt_ref, la_ref, start_ref, final_ref = refs[20:26]
    so_refs, pg_refs = refs[26:28], refs[28:30]
    mine_ref, theirs_ref, ddt_ref, dla_ref = refs[30:34]
    x_s, pre_s, states, cots, weigh = refs[34:]
    z, core = place[0], place[1]
    even = core == 0
    half = HEAD_DIM // 2

    def lanes(k):
        return pl.ds(pl.multiple_of(lax.rem(k - z + DEPTH, DEPTH) * BLOCK, BLOCK), BLOCK)

    def summed(unit, at):
        c0, r1a, r3a, r1b, r3b = sums[unit * 5 : unit * 5 + 5]
        sides = jnp.concatenate(
            [add(r1a[:, at], r3a[:, at]), add(r1b[:, at], r3b[:, at])], axis=0
        )
        return c0[:, at].astype(F32) + sides

    def ordered(mine, theirs):
        return jnp.concatenate(
            [jnp.where(even, mine, theirs), jnp.where(even, theirs, mine)], axis=1
        )

    rows = lax.broadcasted_iota(jnp.int32, (CHUNK, CHUNK), 0)
    cols = lax.broadcasted_iota(jnp.int32, (CHUNK, CHUNK), 1)
    upper = rows <= cols
    dt = dt_ref[...]
    run = dot(la_ref[...], upper.astype(F32), precision=HIGH)
    closing = run[:, CHUNK - 1 :]
    from_start = jnp.exp(run)
    to_end = jnp.exp(closing - run)
    through = jnp.exp(closing)
    run_t = run.T

    for k in range(DEPTH):
        at = lanes(k)
        span = pl.ds(k * CHUNK, CHUNK)
        pre = ordered(summed(0, at), summed(1, at))
        grad = ordered(summed(2, at), summed(3, at)).astype(BF16)
        pre_s[:, span] = pre
        signal = (pre / (1.0 + jnp.exp(-pre))).astype(BF16)
        x_s[0, :, span] = signal
        x_s[1, :, span] = grad
        carried = (signal.astype(F32) * (dt[k : k + 1] * to_end[k : k + 1])).astype(BF16)
        states[k + 1] = dot(carried, b_ref[span, :])
        arrived = (grad.astype(F32) * from_start[k : k + 1]).astype(BF16)
        cots[k] = dot(arrived, c_ref[span, :])
    states[0] = start_ref[...]
    cots[DEPTH] = final_ref[...]
    for k in range(DEPTH):
        states[k + 1] = states[k + 1] + through[k : k + 1] * states[k]
    for k in reversed(range(DEPTH)):
        cots[k] = cots[k] + through[k : k + 1] * cots[k + 1]

    last = lax.broadcasted_iota(jnp.int32, (1, CHUNK), 1) == CHUNK - 1
    for k in range(DEPTH):
        at = lanes(k)
        span = pl.ds(k * CHUNK, CHUNK)
        signal, grad, pre = x_s[0, :, span], x_s[1, :, span], pre_s[:, span]
        b, c = b_ref[span, :], c_ref[span, :]
        step = dt[k : k + 1]
        rise, fall = from_start[k : k + 1], to_end[k : k + 1]
        signal32, grad32 = signal.astype(F32), grad.astype(F32)
        stepped32 = signal32 * step
        stepped = stepped32.astype(BF16)
        carried = (stepped32 * fall).astype(BF16)
        arrived = (grad32 * rise).astype(BF16)
        state, cot = states[k].astype(BF16), cots[k + 1].astype(BF16)
        decay = jnp.where(
            upper, jnp.exp(jnp.minimum(run[k : k + 1] - run_t[:, k : k + 1], 0.0)), 0.0
        )
        mixing = (dot(b, c, NT) * decay).astype(BF16)
        out = dot(stepped, mixing) + dot(state, c, NT) * rise
        back = dot(grad, mixing, NT) + dot(cot, b, NT) * fall
        pair = (dot(stepped, grad, TN) * decay).astype(BF16)
        b_grad = dot(pair, c) + dot(carried, cot, TN)
        c_grad = dot(pair, b, TN) + dot(arrived, state, TN)
        sig = 1.0 / (1.0 + jnp.exp(-pre))
        pre_grad = (back * step) * (sig * (1.0 + pre * (1.0 - sig)))
        for value, targets in ((out, so_refs), (pre_grad, pg_refs)):
            left, right = value[:, :BLOCK], value[:, BLOCK:]
            targets[0][:, at] = jnp.where(even, left, right).astype(BF16)
            targets[1][:, at] = jnp.where(even, right, left).astype(BF16)
        low = jnp.concatenate([b_grad[:, :BLOCK], c_grad[:, :BLOCK]], axis=1)
        high = jnp.concatenate([b_grad[:, BLOCK:], c_grad[:, BLOCK:]], axis=1)
        mine_ref[span, :] = jnp.where(even, low, high).astype(BF16)
        theirs_ref[span, :] = jnp.where(even, high, low).astype(BF16)
        step_grad = jnp.sum(signal32 * back, axis=0, keepdims=True)
        ddt_ref[k : k + 1, :] = step_grad
        anchor = jnp.sum(states[k + 1] * cots[k + 1])
        turn = jnp.sum(grad32 * out, axis=0, keepdims=True) - step * step_grad
        weigh[k : k + 1, :] = turn + jnp.where(last, anchor, 0.0)
    dla_ref[...] = dot(weigh[...], (rows >= cols).astype(F32), precision=HIGH)


def run_scan(place, sums, b, c, dt, la, start, final):
    tokens = DEPTH * CHUNK
    half_tokens = tokens // 2
    vm = pl.BlockSpec(memory_space=pltpu.VMEM)
    shapes = (
        [jax.ShapeDtypeStruct((HEAD_DIM, half_tokens), BF16)] * 4
        + [jax.ShapeDtypeStruct((tokens, STATE), BF16)] * 2
        + [jax.ShapeDtypeStruct((DEPTH, CHUNK), F32)] * 2
    )
    return pl.pallas_call(
        scan_kernel,
        out_shape=shapes,
        in_specs=[pl.BlockSpec(memory_space=pltpu.SMEM)] + [vm] * 26,
        out_specs=[vm] * 8,
        scratch_shapes=[
            pltpu.VMEM((2, HEAD_DIM, tokens), BF16),
            pltpu.VMEM((HEAD_DIM, tokens), F32),
            pltpu.VMEM((DEPTH + 1, HEAD_DIM, STATE), F32),
            pltpu.VMEM((DEPTH + 1, HEAD_DIM, STATE), F32),
            pltpu.VMEM((DEPTH, CHUNK), F32),
        ],
        compiler_params=pltpu.CompilerParams(vmem_limit_bytes=40 * 1024 * 1024),
        cost_estimate=pl.CostEstimate(
            flops=2_000_000_000, bytes_accessed=10_000_000, transcendentals=1_000_000
        ),
    )(place, *sums, b, c, dt, la, start, final)


def rolled(a, x, y):
    grid = a.reshape(SIDE, SIDE, HEAD_DIM, a.shape[1])
    return jnp.roll(jnp.roll(grid, -x, axis=0), -y, axis=1)


def body(
    layer_input,
    output_grad,
    inproj_weight,
    outproj_weight,
    input_coeffs,
    output_coeffs,
    step_sizes,
    log_decay,
    state_start,
    state_grad,
):
    row = lax.axis_index("row")
    column = lax.axis_index("col")
    x, y = row // SIDE, row % SIDE
    z, core = column // 2, column % 2
    group = z * STATE
    coeffs = jnp.concatenate(
        [
            lax.dynamic_slice_in_dim(input_coeffs, group, STATE, 1),
            lax.dynamic_slice_in_dim(output_coeffs, group, STATE, 1),
        ],
        axis=1,
    )
    coeffs = lax.all_gather(coeffs, "row", axis=0, tiled=True)
    rates = lax.all_gather(jnp.concatenate([step_sizes, log_decay], axis=0), "row")
    rates = lax.dynamic_index_in_dim(
        rates.reshape(16, 2, 16, BLOCK), row, 2, keepdims=False
    )
    rates = rates.transpose(1, 0, 2).reshape(2, DEPTH, CHUNK)
    start = lax.dynamic_index_in_dim(state_start, row, 0, False)
    final = lax.dynamic_index_in_dim(state_grad, row, 0, False)

    in_rows = rolled(inproj_weight.T, x, y)
    out_rows = rolled(outproj_weight, x, y)

    def by_y(grid):
        return [grid[:, d].reshape(SIDE * HEAD_DIM, -1) for d in range(SIDE)]

    def by_x(grid):
        return [grid[d].reshape(SIDE * HEAD_DIM, -1) for d in range(SIDE)]

    input_mine = gather_z(layer_input)
    input_theirs = swap_core(input_mine)
    grad_mine = gather_z(output_grad)
    grad_theirs = swap_core(grad_mine)

    sums = []
    for grid, mine, theirs in (
        (in_rows, input_mine, input_theirs),
        (out_rows, grad_mine, grad_theirs),
    ):
        for parts in (
            reduce_grid(by_y(grid), mine, shift_y, shift_x),
            reduce_grid(by_x(grid), theirs, shift_x, shift_y),
        ):
            (c0a, r1a, r3a), (c0b, r1b, r3b) = parts
            sums.extend([jnp.concatenate([c0a, c0b], axis=0), r1a, r3a, r1b, r3b])

    place = jnp.stack([z, core]).astype(jnp.int32)
    so_mine, so_theirs, pg_mine, pg_theirs, mine, theirs, ddt, dla = run_scan(
        place, sums, coeffs[:, :STATE], coeffs[:, STATE:], rates[0], rates[1], start, final
    )

    inner = SIDE * SIDE * HEAD_DIM
    scan_output = jnp.concatenate([so_mine, so_theirs], axis=1)
    pre_grad = jnp.concatenate([pg_mine, pg_theirs], axis=1)
    pre_grad = gather_grid(pre_grad, shift_y, shift_x, y, x, 1).reshape(inner, -1)
    scan_output = gather_grid(scan_output, shift_x, shift_y, x, y, 0).reshape(inner, -1)

    half_tokens = DEPTH * BLOCK
    update_theirs = lax.dot_general(
        pre_grad[:, half_tokens:],
        inproj_weight,
        (((0,), (1,)), ((), ())),
        preferred_element_type=F32,
    ).astype(BF16)
    update_mine = lax.dot_general(
        pre_grad[:, :half_tokens],
        inproj_weight,
        (((0,), (1,)), ((), ())),
        preferred_element_type=F32,
    )
    update = update_mine + swap_core(update_theirs).astype(F32)
    chunks = [update[d * BLOCK : (d + 1) * BLOCK] for d in range(DEPTH)]
    input_grad = scatter_z(chunks).astype(BF16)

    input_all = jnp.concatenate([input_mine, input_theirs], axis=0)
    grad_all = jnp.concatenate([grad_mine, grad_theirs], axis=0)
    outproj_grad = lax.dot_general(
        scan_output, grad_all, (((1,), (0,)), ((), ())), preferred_element_type=F32
    )
    inproj_grad = lax.dot_general(
        input_all, pre_grad, (((0,), (1,)), ((), ())), preferred_element_type=F32
    )

    both = (mine.astype(F32) + swap_core(theirs).astype(F32)).astype(BF16)
    both = lax.psum_scatter(both, "row", scatter_dimension=0, tiled=True).astype(F32)
    incoeff_grad, outcoeff_grad = both[:, :BLOCK], both[:, BLOCK:]

    tokens = DEPTH * CHUNK
    lines = jnp.stack([ddt.reshape(tokens), dla.reshape(tokens)])
    lines = lax.all_gather(lines, "row")
    lines = lax.dynamic_slice_in_dim(lines, row * BLOCK, BLOCK, 2)
    return (
        input_grad,
        inproj_grad,
        outproj_grad,
        incoeff_grad,
        outcoeff_grad,
        lines[:, 0],
        lines[:, 1],
    )


def solution(mesh):
    return jax.shard_map(
        body,
        mesh=mesh,
        in_specs=(
            P("col", "row"),
            P("col", "row"),
            P("row", "col"),
            P("col", "row"),
            P("row", None),
            P("row", None),
            P("col", "row"),
            P("col", "row"),
            P("col", None, None),
            P("col", None, None),
        ),
        out_specs=(
            P("col", "row"),
            P("row", "col"),
            P("col", "row"),
            P("row", "col"),
            P("row", "col"),
            P("col", "row"),
            P("col", "row"),
        ),
        check_vma=False,
    )
```

```python
import functools

import jax
import jax.numpy as jnp
from jax import lax
from jax.experimental import pallas as pl
from jax.experimental.pallas import tpu as pltpu
from jax.sharding import PartitionSpec as P

HEAD_DIM = 64
STATE = 256
SIDE = 4
DEPTH = 8
BLOCK = 128
CHUNK = 256
F32 = jnp.float32
BF16 = jnp.bfloat16
VM = pl.BlockSpec(memory_space=pltpu.VMEM)
SM = pl.BlockSpec(memory_space=pltpu.SMEM)
ROOM = pltpu.CompilerParams(vmem_limit_bytes=40 * 1024 * 1024)


def shift_y(a, d):
    pairs = [(x * 4 + y, x * 4 + (y + d) % 4) for x in range(4) for y in range(4)]
    return lax.ppermute(a, "row", pairs)


def shift_x(a, d):
    pairs = [(x * 4 + y, (x + d) % 4 * 4 + y) for x in range(4) for y in range(4)]
    return lax.ppermute(a, "row", pairs)


def shift_z(a, d):
    pairs = [(z * 2 + c, (z + d) % 8 * 2 + c) for z in range(8) for c in range(2)]
    return lax.ppermute(a, "col", pairs)


def swap_core(a):
    return lax.ppermute(a, "col", [(i, i ^ 1) for i in range(16)])


def add(*terms):
    total = terms[0].astype(F32)
    for term in terms[1:]:
        total = total + term.astype(F32)
    return total


def gather_z(own):
    half = own.shape[0] // 2
    up1, down1 = shift_z(own, 1), shift_z(own, -1)
    up2, down2 = shift_z(up1, 1), shift_z(down1, -1)
    up3, down3 = shift_z(up2, 1), shift_z(down2, -1)
    far = (shift_z(up3[:half], 1), shift_z(down3[half:], -1))
    return [own, down1, down2, down3, *far, up3, up2, up1]


def bump_kernel(first, base, extra, *refs):
    out = refs[-1]
    out[...] = base[...]
    half = extra.shape[0]
    at = pl.ds(first, half)
    out[at] = add(base[at], extra[...]).astype(BF16)


def bump(base, extra, first, *waits):
    return pl.pallas_call(
        functools.partial(bump_kernel, first),
        out_shape=jax.ShapeDtypeStruct(base.shape, BF16),
        in_specs=[VM, VM] + [pl.BlockSpec(memory_space=pl.ANY)] * len(waits),
        out_specs=VM,
        compiler_params=ROOM,
    )(base, extra, *waits)


def reduce_ring(chunks, shift, *waits):
    c0, c1, c2a, c2b, c3 = chunks
    far_a, far_b = shift(c2a, 1), shift(c2b, -1)
    half = c2a.shape[0]
    c1 = bump(c1, far_a, 0, *waits)
    c3 = bump(c3, far_b, half, *waits)
    return c0, shift(c1, 1), shift(c3, -1)


def reduce_grid(chunks, first, second, *waits):
    own = add(*reduce_ring(chunks, first, *waits)).astype(BF16)
    return reduce_ring((own[0], own[1], own[2][:1], own[2][1:], own[3]), second)


def cut_kernel(first, base, *refs):
    out = refs[-1]
    out[...] = base[pl.ds(first, out.shape[0])]


def cut(base, first, *waits):
    half = base.shape[0] // 2
    return pl.pallas_call(
        functools.partial(cut_kernel, first * half),
        out_shape=jax.ShapeDtypeStruct((half, *base.shape[1:]), BF16),
        in_specs=[VM] + [pl.BlockSpec(memory_space=pl.ANY)] * len(waits),
        out_specs=VM,
        compiler_params=ROOM,
    )(base, *waits)


def gather_ring(own, shift, *waits):
    up, down = shift(own, 1), shift(own, -1)
    return own, down, shift(cut(up, 0, *waits), 1), shift(cut(down, 1, *waits), -1), up


def scatter_z(total):
    rows = total.shape[0] // DEPTH
    half = rows // 2
    chunks = [total[d * rows : (d + 1) * rows] for d in range(DEPTH)]
    up = shift_z(chunks[4][:half], 1)
    down = shift_z(chunks[4][half:], -1)
    up = first = bump(chunks[3], up, 0)
    up, down = shift_z(up, 1), shift_z(bump(chunks[5], down, half), -1)
    up = second = bump(chunks[2], up, 0)
    up, down = shift_z(up, 1), shift_z(bump(chunks[6], down, 0), -1)
    up = shift_z(bump(chunks[1], up, 0), 1)
    down = shift_z(bump(chunks[7], down, 0), -1)
    return add(chunks[0], up, down).astype(BF16), first, second


def dot(a, b, dims=((1,), (0,)), precision=None):
    return lax.dot_general(a, b, (dims, ((), ())), preferred_element_type=F32, precision=precision)


NT = ((1,), (1,))
TN = ((0,), (0,))
HIGH = lax.Precision.HIGHEST


def turn(at, d):
    return lax.rem(at + d, SIDE)


def project_kernel(y_first, pack, place, *refs):
    x, y = place[2], place[3]
    if pack:
        in_pieces, grad_pieces, refs = refs[:9], refs[9:18], refs[18:]
        in_w, grad_w, in_ref, grad_ref, c0, c1, c2a, c2b, c3 = refs
        for pieces, target in ((in_pieces, in_ref), (grad_pieces, grad_ref)):
            row = 0
            for piece in pieces:
                target[row : row + piece.shape[0], :] = piece[...]
                row += piece.shape[0]
    else:
        in_ref, grad_ref, in_w, grad_w, c0, c1, c2a, c2b, c3 = refs

    def one(tile, carry):
        span = pl.ds(pl.multiple_of(tile * CHUNK, CHUNK), CHUNK)
        for which, (tokens_ref, w_ref) in enumerate(((in_ref, in_w), (grad_ref, grad_w))):
            tokens = tokens_ref[span, :]
            for d in range(SIDE):
                pieces = []
                for i in range(SIDE):
                    at_x, at_y = (turn(x, i), turn(y, d)) if y_first else (turn(x, d), turn(y, i))
                    start = pl.multiple_of((at_x * SIDE + at_y) * HEAD_DIM, HEAD_DIM)
                    pieces.append(w_ref[pl.ds(start, HEAD_DIM), :])
                part = dot(jnp.concatenate(pieces, axis=0), tokens, NT).astype(BF16)
                for i in range(SIDE):
                    if d == 2:
                        target, at = (c2a, i) if i < 2 else (c2b, i - 2)
                    else:
                        target, at = ((c0, c1, None, c3)[d], i)
                    rows = part[i * HEAD_DIM : (i + 1) * HEAD_DIM]
                    target[at, which, :, span] = rows
        return carry

    lax.fori_loop(0, DEPTH * BLOCK // CHUNK, one, 0)


def project(place, inputs, grads, in_w, grad_w, y_first):
    pack = len(inputs) > 1
    tokens, width = DEPTH * BLOCK, in_w.shape[1]
    packed = jax.ShapeDtypeStruct((tokens, width), BF16)
    chunk = jax.ShapeDtypeStruct((SIDE, 2, HEAD_DIM, tokens), BF16)
    half = jax.ShapeDtypeStruct((SIDE // 2, 2, HEAD_DIM, tokens), BF16)
    shapes = [packed] * (2 * pack) + [chunk, chunk, half, half, chunk]
    return pl.pallas_call(
        functools.partial(project_kernel, y_first, pack),
        out_shape=shapes,
        in_specs=[SM] + [VM] * (len(inputs) + len(grads) + 2),
        out_specs=[VM] * len(shapes),
        compiler_params=ROOM,
        cost_estimate=pl.CostEstimate(
            flops=4 * 1024 * tokens * width, bytes_accessed=12_000_000, transcendentals=0
        ),
    )(place, *inputs, *grads, in_w, grad_w)


def line_kernel(axis, place, own, down, far_a, far_b, up, out):
    at = place[axis]
    half = own.shape[0] // 2
    out[at] = own[...]
    out[turn(at, 1)] = down[...]
    out[turn(at, 2), :half] = far_a[...]
    out[turn(at, 2), half:] = far_b[...]
    out[turn(at, 3)] = up[...]


def line_up(place, pieces, axis):
    return pl.pallas_call(
        functools.partial(line_kernel, axis),
        out_shape=jax.ShapeDtypeStruct((SIDE, *pieces[0].shape), BF16),
        in_specs=[SM] + [VM] * 5,
        out_specs=VM,
        compiler_params=ROOM,
    )(place, *pieces)


def update_kernel(y_first, place, own, down, far_a, far_b, up, w_ref, grads, outs, update):
    x, y = place[2], place[3]
    for ref, d, low in ((own, 0, 0), (down, 1, 0), (far_a, 2, 0), (far_b, 2, 2), (up, 3, 0)):
        for i in range(ref.shape[0]):
            at_x, at_y = (turn(x, d), low + i) if y_first else (low + i, turn(y, d))
            start = pl.multiple_of((at_x * SIDE + at_y) * HEAD_DIM, HEAD_DIM)
            grads[pl.ds(start, HEAD_DIM), :] = ref[i, 0]
            outs[pl.ds(start, HEAD_DIM), :] = ref[i, 1]
    for tile in range(DEPTH * BLOCK // CHUNK):
        span = pl.ds(tile * CHUNK, CHUNK)
        update[span, :] = dot(grads[:, span], w_ref[...], TN).astype(BF16)


def run_update(place, pieces, w, y_first):
    tokens = pieces[0].shape[-1]
    whole = jax.ShapeDtypeStruct((w.shape[0], tokens), BF16)
    return pl.pallas_call(
        functools.partial(update_kernel, y_first),
        out_shape=[whole, whole, jax.ShapeDtypeStruct((tokens, w.shape[1]), BF16)],
        in_specs=[SM] + [VM] * 6,
        out_specs=[VM] * 3,
        compiler_params=ROOM,
        cost_estimate=pl.CostEstimate(
            flops=2 * w.size * tokens, bytes_accessed=6_000_000, transcendentals=0
        ),
    )(place, *pieces, w)


def weight_kernel(turned, a_mine, b_mine, a_theirs, b_theirs, *refs):
    out = refs[-1]
    for tile in range(a_mine.shape[0] // CHUNK):
        span = pl.ds(tile * CHUNK, CHUNK)
        part = dot(a_mine[span, :], b_mine[...]) + dot(a_theirs[span, :], b_theirs[...])
        if turned:
            out[:, span] = part.T
        else:
            out[span, :] = part


def weight_grad(a_mine, b_mine, a_theirs, b_theirs, turned, *waits):
    rows, cols = a_mine.shape[0], b_mine.shape[1]
    return pl.pallas_call(
        functools.partial(weight_kernel, turned),
        out_shape=jax.ShapeDtypeStruct((cols, rows) if turned else (rows, cols), F32),
        in_specs=[VM] * 4 + [pl.BlockSpec(memory_space=pl.ANY)] * len(waits),
        out_specs=VM,
        compiler_params=ROOM,
        cost_estimate=pl.CostEstimate(
            flops=4 * rows * cols * a_mine.shape[1], bytes_accessed=8_000_000, transcendentals=0
        ),
    )(a_mine, b_mine, a_theirs, b_theirs, *waits)


def scan_kernel(place, *refs):
    sums = refs[:6]
    coeff_ref, dt_ref, la_ref, start_ref, final_ref = refs[6:11]
    own_mine, own_theirs, mine_ref, theirs_ref = refs[11:15]
    x_s, pre_s, states, cots, weigh, steps = refs[15:]
    z, core = place[0], place[1]
    even = core == 0

    def lanes(k):
        return pl.ds(pl.multiple_of(lax.rem(k - z + DEPTH, DEPTH) * BLOCK, BLOCK), BLOCK)

    def summed(unit, which, at):
        return add(*(ref[which, :, at] for ref in sums[unit * 3 : unit * 3 + 3]))

    def ordered(mine, theirs):
        return jnp.concatenate(
            [jnp.where(even, mine, theirs), jnp.where(even, theirs, mine)], axis=1
        )

    def coeffs(k, which):
        block = coeff_ref[2 * k : 2 * k + 2, :BLOCK, which * STATE : (which + 1) * STATE]
        return block.reshape(CHUNK, STATE)

    rows = lax.broadcasted_iota(jnp.int32, (CHUNK, CHUNK), 0)
    cols = lax.broadcasted_iota(jnp.int32, (CHUNK, CHUNK), 1)
    upper = rows <= cols
    dt = dt_ref[...]
    run = dot(la_ref[...], upper.astype(F32), precision=HIGH)
    closing = run[:, CHUNK - 1 :]
    from_start = jnp.exp(run)
    to_end = jnp.exp(closing - run)
    through = jnp.exp(closing)
    run_t = run.T

    for k in range(DEPTH):
        at = lanes(k)
        span = pl.ds(k * CHUNK, CHUNK)
        pre = ordered(summed(0, 0, at), summed(1, 0, at))
        grad = ordered(summed(0, 1, at), summed(1, 1, at)).astype(BF16)
        pre_s[:, span] = pre
        signal = (pre / (1.0 + jnp.exp(-pre))).astype(BF16)
        x_s[0, :, span] = signal
        x_s[1, :, span] = grad
        carried = (signal.astype(F32) * (dt[k : k + 1] * to_end[k : k + 1])).astype(BF16)
        states[k + 1] = dot(carried, coeffs(k, 0))
        arrived = (grad.astype(F32) * from_start[k : k + 1]).astype(BF16)
        cots[k] = dot(arrived, coeffs(k, 1))
    states[0] = start_ref[...]
    cots[DEPTH] = final_ref[...]
    for k in range(DEPTH):
        states[k + 1] = states[k + 1] + through[k : k + 1] * states[k]
    for k in reversed(range(DEPTH)):
        cots[k] = cots[k] + through[k : k + 1] * cots[k + 1]

    last = lax.broadcasted_iota(jnp.int32, (1, CHUNK), 1) == CHUNK - 1
    for k in range(DEPTH):
        at = lanes(k)
        span = pl.ds(k * CHUNK, CHUNK)
        signal, grad, pre = x_s[0, :, span], x_s[1, :, span], pre_s[:, span]
        b, c = coeffs(k, 0), coeffs(k, 1)
        step = dt[k : k + 1]
        rise, fall = from_start[k : k + 1], to_end[k : k + 1]
        signal32, grad32 = signal.astype(F32), grad.astype(F32)
        stepped32 = signal32 * step
        stepped = stepped32.astype(BF16)
        carried = (stepped32 * fall).astype(BF16)
        arrived = (grad32 * rise).astype(BF16)
        state, cot = states[k].astype(BF16), cots[k + 1].astype(BF16)
        decay = jnp.where(
            upper, jnp.exp(jnp.minimum(run[k : k + 1] - run_t[:, k : k + 1], 0.0)), 0.0
        )
        mixing = (dot(b, c, NT) * decay).astype(BF16)
        out = dot(stepped, mixing) + dot(state, c, NT) * rise
        back = dot(grad, mixing, NT) + dot(cot, b, NT) * fall
        pair = (dot(stepped, grad, TN) * decay).astype(BF16)
        b_grad = dot(pair, c) + dot(carried, cot, TN)
        c_grad = dot(pair, b, TN) + dot(arrived, state, TN)
        sig = 1.0 / (1.0 + jnp.exp(-pre))
        pre_grad = (back * step) * (sig * (1.0 + pre * (1.0 - sig)))
        for which, value in enumerate((pre_grad, out)):
            left, right = value[:, :BLOCK], value[:, BLOCK:]
            own_mine[which, :, at] = jnp.where(even, left, right).astype(BF16)
            own_theirs[which, :, at] = jnp.where(even, right, left).astype(BF16)
        low = jnp.concatenate([b_grad[:, :BLOCK], c_grad[:, :BLOCK]], axis=1)
        high = jnp.concatenate([b_grad[:, BLOCK:], c_grad[:, BLOCK:]], axis=1)
        for h in range(2):
            rows_h = slice(h * BLOCK, (h + 1) * BLOCK)
            mine_ref[2 * k + h, :BLOCK, :] = jnp.where(even, low[rows_h], high[rows_h]).astype(BF16)
            theirs_ref[2 * k + h, :BLOCK, :] = jnp.where(
                even, high[rows_h], low[rows_h]
            ).astype(BF16)
        step_grad = jnp.sum(signal32 * back, axis=0, keepdims=True)
        steps[k : k + 1, :] = step_grad
        anchor = jnp.sum(states[k + 1] * cots[k + 1])
        turned = jnp.sum(grad32 * out, axis=0, keepdims=True) - step * step_grad
        weigh[k : k + 1, :] = turned + jnp.where(last, anchor, 0.0)
    decays = dot(weigh[...], (rows >= cols).astype(F32), precision=HIGH)
    blank = jnp.zeros((16, STATE), F32)
    which_row = lax.broadcasted_iota(jnp.int32, (16, STATE), 0)
    for k in range(DEPTH):
        for h in range(2):
            span = slice(h * BLOCK, (h + 1) * BLOCK)
            line = jnp.concatenate([steps[k : k + 1, span], decays[k : k + 1, span]], axis=1)
            coarse = line.astype(BF16).astype(F32)
            tile = jnp.where(which_row == 0, coarse, jnp.where(which_row == 1, line - coarse, 0.0))
            mine_ref[2 * k + h, BLOCK:, :] = tile.astype(BF16)
            theirs_ref[2 * k + h, BLOCK:, :] = blank.astype(BF16)


def run_scan(place, sums, coeffs, dt, la, start, final):
    tokens = DEPTH * CHUNK
    half = jax.ShapeDtypeStruct((2, HEAD_DIM, tokens // 2), BF16)
    grads = jax.ShapeDtypeStruct((16, BLOCK + 16, STATE), BF16)
    return pl.pallas_call(
        scan_kernel,
        out_shape=[half, half, grads, grads],
        in_specs=[SM] + [VM] * 11,
        out_specs=[VM] * 4,
        scratch_shapes=[
            pltpu.VMEM((2, HEAD_DIM, tokens), BF16),
            pltpu.VMEM((HEAD_DIM, tokens), F32),
            pltpu.VMEM((DEPTH + 1, HEAD_DIM, STATE), F32),
            pltpu.VMEM((DEPTH + 1, HEAD_DIM, STATE), F32),
            pltpu.VMEM((DEPTH, CHUNK), F32),
            pltpu.VMEM((DEPTH, CHUNK), F32),
        ],
        compiler_params=ROOM,
        cost_estimate=pl.CostEstimate(
            flops=2_000_000_000, bytes_accessed=10_000_000, transcendentals=1_000_000
        ),
    )(place, *sums, coeffs, dt, la, start, final)


def body(
    layer_input,
    output_grad,
    inproj_weight,
    outproj_weight,
    input_coeffs,
    output_coeffs,
    step_sizes,
    log_decay,
    state_start,
    state_grad,
):
    row = lax.axis_index("row")
    column = lax.axis_index("col")
    x, y = row // SIDE, row % SIDE
    z, core = column // 2, column % 2
    place = jnp.stack([z, core, x, y]).astype(jnp.int32)
    group = z * STATE
    rates = jnp.concatenate([step_sizes, log_decay], axis=0).reshape(8, 2 * STATE)
    coarse = lax.reduce_precision(rates, 8, 7)
    coeffs = jnp.concatenate(
        [
            jnp.concatenate(
                [
                    lax.dynamic_slice_in_dim(input_coeffs, group, STATE, 1),
                    lax.dynamic_slice_in_dim(output_coeffs, group, STATE, 1),
                ],
                axis=1,
            ),
            coarse.astype(BF16),
            (rates - coarse).astype(BF16),
        ],
        axis=0,
    )
    coeffs = lax.all_gather(coeffs, "row", axis=0, tiled=True).reshape(16, BLOCK + 16, 2 * STATE)
    rates = add(coeffs[:, BLOCK : BLOCK + 8], coeffs[:, BLOCK + 8 :]).reshape(16, 2, 16, BLOCK)
    rates = lax.dynamic_index_in_dim(rates, row, 2, keepdims=False)
    rates = rates.transpose(1, 0, 2).reshape(2, DEPTH, CHUNK)
    start = lax.dynamic_index_in_dim(state_start, row, 0, False)
    final = lax.dynamic_index_in_dim(state_grad, row, 0, False)
    in_w = inproj_weight.T

    input_mine, grad_mine, *chunks = project(
        place, gather_z(layer_input), gather_z(output_grad), in_w, outproj_weight, True
    )
    input_theirs, grad_theirs = swap_core(input_mine), swap_core(grad_mine)
    away = project(place, [input_theirs], [grad_theirs], in_w, outproj_weight, False)
    sums = list(reduce_grid(chunks, shift_y, shift_x, away[0]))
    sums.extend(reduce_grid(away, shift_x, shift_y))

    own_mine, own_theirs, mine, theirs = run_scan(
        place, sums, coeffs, rates[0], rates[1], start, final
    )
    both = add(mine, swap_core(theirs)).astype(BF16)
    both = lax.all_to_all(both, "row", 0, 0)

    line_theirs = line_up(place, gather_ring(own_theirs, shift_x), 2)
    line_mine = line_up(place, gather_ring(own_mine, shift_y), 3)
    pg_theirs, so_theirs, update_theirs = run_update(
        place, gather_ring(line_theirs, shift_y, both), in_w, False
    )
    update_theirs = swap_core(update_theirs)
    pg_mine, so_mine, update_mine = run_update(
        place, gather_ring(line_mine, shift_x, both), in_w, True
    )
    input_grad, first, second = scatter_z(add(update_mine, update_theirs).astype(BF16))
    inproj_grad = weight_grad(pg_mine, input_mine, pg_theirs, input_theirs, True, first)
    outproj_grad = weight_grad(so_mine, grad_mine, so_theirs, grad_theirs, False, second)

    coeff_grads = jnp.sum(both[:, :BLOCK].astype(F32), axis=0)
    lines = add(both[:, BLOCK], both[:, BLOCK + 1])
    return (
        input_grad,
        inproj_grad,
        outproj_grad,
        coeff_grads[:, :BLOCK],
        coeff_grads[:, BLOCK:],
        lines[:, :BLOCK],
        lines[:, BLOCK:],
    )


def solution(mesh):
    return jax.shard_map(
        body,
        mesh=mesh,
        in_specs=(
            P("col", "row"),
            P("col", "row"),
            P("row", "col"),
            P("col", "row"),
            P("row", None),
            P("row", None),
            P("col", "row"),
            P("col", "row"),
            P("col", None, None),
            P("col", None, None),
        ),
        out_specs=(
            P("col", "row"),
            P("row", "col"),
            P("col", "row"),
            P("row", "col"),
            P("row", "col"),
            P("col", "row"),
            P("col", "row"),
        ),
        check_vma=False,
    )
```

```python
import functools

import jax
import jax.numpy as jnp
from jax import lax
from jax.experimental import pallas as pl
from jax.experimental.pallas import tpu as pltpu
from jax.sharding import PartitionSpec as P

HEAD_DIM = 64
STATE = 256
SIDE = 4
DEPTH = 8
BLOCK = 128
CHUNK = 256
F32 = jnp.float32
BF16 = jnp.bfloat16
VM = pl.BlockSpec(memory_space=pltpu.VMEM)
SM = pl.BlockSpec(memory_space=pltpu.SMEM)
ANY = pl.BlockSpec(memory_space=pl.ANY)
ROOM = pltpu.CompilerParams(vmem_limit_bytes=40 * 1024 * 1024)


def shift_y(a, d):
    pairs = [(x * 4 + y, x * 4 + (y + d) % 4) for x in range(4) for y in range(4)]
    return lax.ppermute(a, "row", pairs)


def shift_x(a, d):
    pairs = [(x * 4 + y, (x + d) % 4 * 4 + y) for x in range(4) for y in range(4)]
    return lax.ppermute(a, "row", pairs)


def shift_z(a, d):
    pairs = [(z * 2 + c, (z + d) % 8 * 2 + c) for z in range(8) for c in range(2)]
    return lax.ppermute(a, "col", pairs)


def swap_core(a):
    return lax.ppermute(a, "col", [(i, i ^ 1) for i in range(16)])


def add(*terms):
    total = terms[0].astype(F32)
    for term in terms[1:]:
        total = total + term.astype(F32)
    return total


def gather_z(own):
    half = own.shape[0] // 2
    up1, down1 = shift_z(own, 1), shift_z(own, -1)
    up2, down2 = shift_z(up1, 1), shift_z(down1, -1)
    up3, down3 = shift_z(up2, 1), shift_z(down2, -1)
    far = (shift_z(up3[:half], 1), shift_z(down3[half:], -1))
    return [own, down1, down2, down3, *far, up3, up2, up1]


def bump_kernel(first, base, extra, *refs):
    out = refs[-1]
    if extra.shape == base.shape:
        out[...] = add(base[...], extra[...]).astype(BF16)
    else:
        out[...] = base[...]
        at = pl.ds(first, extra.shape[0])
        out[at] = add(base[at], extra[...]).astype(BF16)


def bump(base, extra, first, *waits):
    return pl.pallas_call(
        functools.partial(bump_kernel, first),
        out_shape=jax.ShapeDtypeStruct(base.shape, BF16),
        in_specs=[VM, VM] + [ANY] * len(waits),
        out_specs=VM,
        compiler_params=ROOM,
    )(base, extra, *waits)


def own_kernel(c0, first_up, second_up, first_down, second_down, *refs):
    outs = refs[-5:]
    half = first_up.shape[0]
    near = add(c0[:half], first_up[...], first_down[...]).astype(BF16)
    away = add(c0[half:], second_up[...], second_down[...]).astype(BF16)
    outs[0][...] = near[0]
    outs[1][...] = near[1]
    outs[2][...] = away[0, :1]
    outs[3][...] = away[0, 1:]
    outs[4][...] = away[1]


def own_sum(c0, pieces, *waits):
    whole = jax.ShapeDtypeStruct(c0.shape[1:], BF16)
    half = jax.ShapeDtypeStruct((1, *c0.shape[2:]), BF16)
    return pl.pallas_call(
        own_kernel,
        out_shape=[whole, whole, half, half, whole],
        in_specs=[VM] * 5 + [ANY] * len(waits),
        out_specs=[VM] * 5,
        compiler_params=ROOM,
    )(c0, *pieces, *waits)


def reduce_pair(units, shifts, *waits):
    far, free = [], []
    for (c0, c1a, c1b, c2a, c2b, c3a, c3b), shift in zip(units, shifts):
        far.append((shift(c2a, 1), shift(c2b, -1)))
        free.append((shift(c1b, 1), shift(c3a, -1)))
    sums = []
    for i, shift in enumerate(shifts):
        c0, c1a, c1b, c2a, c2b, c3a, c3b = units[i]
        other = far[1 - i]
        last_up = shift(bump(c1a, far[i][0], 0, *other), 1)
        last_down = shift(bump(c3b, far[i][1], 0, *other), -1)
        sums.append((c0, (last_up, free[i][0], free[i][1], last_down)))
    return [own_sum(c0, pieces, *waits) for c0, pieces in sums]


def reduce_small(units, shifts):
    far = [
        (shift(c2a, 1), shift(c2b, -1))
        for (c0, c1, c2a, c2b, c3), shift in zip(units, shifts)
    ]
    parts = []
    for i, shift in enumerate(shifts):
        c0, c1, c2a, c2b, c3 = units[i]
        other = far[1 - i]
        up = shift(bump(c1, far[i][0], 0, *other), 1)
        down = shift(bump(c3, far[i][1], 1, *other), -1)
        parts.append((c0, up, down))
    return parts


def cut_kernel(first, base, *refs):
    out = refs[-1]
    out[...] = base[pl.ds(first, out.shape[0])]


def cut(base, first, *waits):
    half = base.shape[0] // 2
    return pl.pallas_call(
        functools.partial(cut_kernel, first * half),
        out_shape=jax.ShapeDtypeStruct((half, *base.shape[1:]), BF16),
        in_specs=[VM] + [ANY] * len(waits),
        out_specs=VM,
        compiler_params=ROOM,
    )(base, *waits)


def gather_small(units, shifts):
    near = [(shift(own, 1), shift(own, -1)) for own, shift in zip(units, shifts)]
    lines = []
    for i, shift in enumerate(shifts):
        (up, down), other = near[i], near[1 - i]
        far = shift(cut(up, 0, *other), 1), shift(cut(down, 1, *other), -1)
        lines.append((units[i], down, *far, up))
    return lines


def gather_pair(units, shifts):
    first = [(shift(lo, 1), shift(hi, -1)) for (lo, hi), shift in zip(units, shifts)]
    rest = [(shift(hi, 1), shift(lo, -1)) for (lo, hi), shift in zip(units, shifts)]
    far = [(shift(up, 1), shift(down, -1)) for (up, down), shift in zip(first, shifts)]
    return [
        (lo, hi, down_lo, down_hi, far_lo, far_hi, up_lo, up_hi)
        for (lo, hi), (up_lo, down_hi), (up_hi, down_lo), (far_lo, far_hi) in zip(
            units, first, rest, far
        )
    ]


def scatter_z(total, *waits):
    rows = total.shape[0] // DEPTH
    half = rows // 2
    chunks = [total[d * rows : (d + 1) * rows] for d in range(DEPTH)]
    up = shift_z(chunks[4][:half], 1)
    down = shift_z(chunks[4][half:], -1)
    up = first = bump(chunks[3], up, 0)
    up, down = shift_z(up, 1), shift_z(bump(chunks[5], down, half), -1)
    up = second = bump(chunks[2], up, 0)
    up, down = shift_z(up, 1), shift_z(bump(chunks[6], down, 0), -1)
    up = shift_z(bump(chunks[1], up, 0, *waits), 1)
    down = shift_z(bump(chunks[7], down, 0), -1)
    return add(chunks[0], up, down).astype(BF16), first, second


def dot(a, b, dims=((1,), (0,)), precision=None):
    return lax.dot_general(a, b, (dims, ((), ())), preferred_element_type=F32, precision=precision)


NT = ((1,), (1,))
TN = ((0,), (0,))
HIGH = lax.Precision.HIGHEST


def turn(at, d):
    return lax.rem(at + d, SIDE)


def pack_kernel(*refs):
    out = refs[-1]
    pieces = refs[:18]
    for which in range(2):
        row = 0
        for piece in pieces[which * 9 : which * 9 + 9]:
            out[which, row : row + piece.shape[0], :] = piece[...]
            row += piece.shape[0]


def pack(inputs, grads, *waits):
    shape = (2, DEPTH * BLOCK, inputs[0].shape[1])
    return pl.pallas_call(
        pack_kernel,
        out_shape=jax.ShapeDtypeStruct(shape, BF16),
        in_specs=[VM] * 18 + [ANY] * len(waits),
        out_specs=VM,
        compiler_params=ROOM,
    )(*inputs, *grads, *waits)


def project_kernel(y_first, place, tokens_ref, in_w, grad_w, c0, c1a, c1b, c2a, c2b, c3a, c3b):
    x, y = place[2], place[3]
    halves = ((c0, c0), (c1a, c1b), (c2a, c2b), (c3a, c3b))

    def one(tile, carry):
        span = pl.ds(pl.multiple_of(tile * CHUNK, CHUNK), CHUNK)
        for which, w_ref in enumerate((in_w, grad_w)):
            tokens = tokens_ref[which, span, :]
            for d in range(SIDE):
                pieces = []
                for i in range(SIDE):
                    at_x, at_y = (turn(x, i), turn(y, d)) if y_first else (turn(x, d), turn(y, i))
                    start = pl.multiple_of((at_x * SIDE + at_y) * HEAD_DIM, HEAD_DIM)
                    pieces.append(w_ref[pl.ds(start, HEAD_DIM), :])
                part = dot(jnp.concatenate(pieces, axis=0), tokens, NT).astype(BF16)
                for i in range(SIDE):
                    rows = part[i * HEAD_DIM : (i + 1) * HEAD_DIM]
                    halves[d][i // 2][i if d == 0 else i % 2, which, :, span] = rows
        return carry

    lax.fori_loop(0, DEPTH * BLOCK // CHUNK, one, 0)


def project(place, tokens, in_w, grad_w, y_first):
    count, width = tokens.shape[1:]
    chunk = jax.ShapeDtypeStruct((SIDE, 2, HEAD_DIM, count), BF16)
    half = jax.ShapeDtypeStruct((SIDE // 2, 2, HEAD_DIM, count), BF16)
    return pl.pallas_call(
        functools.partial(project_kernel, y_first),
        out_shape=[chunk] + [half] * 6,
        in_specs=[SM] + [VM] * 3,
        out_specs=[VM] * 7,
        compiler_params=ROOM,
        cost_estimate=pl.CostEstimate(
            flops=4 * 1024 * count * width, bytes_accessed=10_000_000, transcendentals=0
        ),
    )(place, tokens, in_w, grad_w)


def line_kernel(axis, place, own, down, far_a, far_b, up, *refs):
    outs = refs[-2:]
    at = place[axis]
    for slot in range(SIDE):
        d = lax.rem(slot - at + SIDE, SIDE)
        target = outs[slot // 2].at[slot % 2]
        far = jnp.concatenate([far_a[...], far_b[...]], axis=0)
        near = jnp.where(d == 0, own[...], down[...])
        away = jnp.where(d == 2, far, up[...])
        target[...] = jnp.where(d < 2, near, away)


def line_up(place, pieces, axis, *waits):
    half = jax.ShapeDtypeStruct((SIDE // 2, *pieces[0].shape), BF16)
    return pl.pallas_call(
        functools.partial(line_kernel, axis),
        out_shape=[half, half],
        in_specs=[SM] + [VM] * 5 + [ANY] * len(waits),
        out_specs=[VM] * 2,
        compiler_params=ROOM,
    )(place, *pieces, *waits)


def update_kernel(y_first, place, *refs):
    x, y = place[2], place[3]
    w_ref, (grads, outs, update) = refs[8], refs[-3:]
    for n, ref in enumerate(refs[:8]):
        d = n // 2
        for i in range(2):
            slot = n % 2 * 2 + i
            at_x, at_y = (turn(x, d), slot) if y_first else (slot, turn(y, d))
            start = pl.multiple_of((at_x * SIDE + at_y) * HEAD_DIM, HEAD_DIM)
            grads[pl.ds(start, HEAD_DIM), :] = ref[i, 0]
            outs[pl.ds(start, HEAD_DIM), :] = ref[i, 1]
    for tile in range(DEPTH * BLOCK // CHUNK):
        span = pl.ds(tile * CHUNK, CHUNK)
        update[span, :] = dot(grads[:, span], w_ref[...], TN).astype(BF16)


def run_update(place, pieces, w, y_first, *waits):
    tokens = pieces[0].shape[-1]
    whole = jax.ShapeDtypeStruct((w.shape[0], tokens), BF16)
    return pl.pallas_call(
        functools.partial(update_kernel, y_first),
        out_shape=[whole, whole, jax.ShapeDtypeStruct((tokens, w.shape[1]), BF16)],
        in_specs=[SM] + [VM] * 9 + [ANY] * len(waits),
        out_specs=[VM] * 3,
        compiler_params=ROOM,
        cost_estimate=pl.CostEstimate(
            flops=2 * w.size * tokens, bytes_accessed=6_000_000, transcendentals=0
        ),
    )(place, *pieces, w, *waits)


def weight_kernel(which, a_mine, b_mine, a_theirs, b_theirs, *refs):
    out = refs[-1]
    for tile in range(a_mine.shape[0] // CHUNK):
        span = pl.ds(tile * CHUNK, CHUNK)
        part = dot(a_mine[span, :], b_mine[which]) + dot(a_theirs[span, :], b_theirs[which])
        if which == 0:
            out[:, span] = part.T
        else:
            out[span, :] = part


def weight_grad(a_mine, b_mine, a_theirs, b_theirs, which, *waits):
    rows, cols = a_mine.shape[0], b_mine.shape[2]
    return pl.pallas_call(
        functools.partial(weight_kernel, which),
        out_shape=jax.ShapeDtypeStruct((rows, cols) if which else (cols, rows), F32),
        in_specs=[VM] * 4 + [ANY] * len(waits),
        out_specs=VM,
        compiler_params=ROOM,
        cost_estimate=pl.CostEstimate(
            flops=4 * rows * cols * a_mine.shape[1], bytes_accessed=8_000_000, transcendentals=0
        ),
    )(a_mine, b_mine, a_theirs, b_theirs, *waits)


def scan_kernel(place, *refs):
    sums = refs[:6]
    coeff_ref, start_ref, final_ref = refs[6:9]
    own_mine, own_theirs, mine_ref, theirs_ref = refs[9:13]
    x_s, pre_s, states, cots, weigh, steps, rates = refs[13:]
    z, core = place[0], place[1]
    even = core == 0

    def lanes(k):
        return pl.ds(pl.multiple_of(lax.rem(k - z + DEPTH, DEPTH) * BLOCK, BLOCK), BLOCK)

    def summed(unit, which, at):
        return add(*(ref[which, :, at] for ref in sums[unit * 3 : unit * 3 + 3]))

    def ordered(mine, theirs):
        return jnp.concatenate(
            [jnp.where(even, mine, theirs), jnp.where(even, theirs, mine)], axis=1
        )

    def coeffs(k, which):
        block = coeff_ref[2 * k : 2 * k + 2, :BLOCK, which * STATE : (which + 1) * STATE]
        return block.reshape(CHUNK, STATE)

    rows = lax.broadcasted_iota(jnp.int32, (CHUNK, CHUNK), 0)
    cols = lax.broadcasted_iota(jnp.int32, (CHUNK, CHUNK), 1)
    upper = rows <= cols
    x, y = place[2], place[3]
    packed_row = lax.broadcasted_iota(jnp.int32, (16, BLOCK), 0)
    for r in range(16):
        tile = coeff_ref[r, BLOCK:, pl.ds(pl.multiple_of(y * BLOCK, BLOCK), BLOCK)].astype(F32)
        for which in range(2):
            chosen = lax.rem(packed_row, 8) == x + 4 * which
            line = jnp.sum(jnp.where(chosen, tile, 0.0), axis=0, keepdims=True)
            rates[which, r // 2 : r // 2 + 1, r % 2 * BLOCK : (r % 2 + 1) * BLOCK] = line
    dt = rates[0]
    run = dot(rates[1], upper.astype(F32), precision=HIGH)
    closing = run[:, CHUNK - 1 :]
    from_start = jnp.exp(run)
    to_end = jnp.exp(closing - run)
    through = jnp.exp(closing)
    run_t = run.T

    for k in range(DEPTH):
        at = lanes(k)
        span = pl.ds(k * CHUNK, CHUNK)
        pre = ordered(summed(0, 0, at), summed(1, 0, at))
        grad = ordered(summed(0, 1, at), summed(1, 1, at)).astype(BF16)
        pre_s[:, span] = pre
        signal = (pre / (1.0 + jnp.exp(-pre))).astype(BF16)
        x_s[0, :, span] = signal
        x_s[1, :, span] = grad
        carried = (signal.astype(F32) * (dt[k : k + 1] * to_end[k : k + 1])).astype(BF16)
        states[k + 1] = dot(carried, coeffs(k, 0))
        arrived = (grad.astype(F32) * from_start[k : k + 1]).astype(BF16)
        cots[k] = dot(arrived, coeffs(k, 1))
    states[0] = start_ref[...]
    cots[DEPTH] = final_ref[...]
    for k in range(DEPTH):
        states[k + 1] = states[k + 1] + through[k : k + 1] * states[k]
    for k in reversed(range(DEPTH)):
        cots[k] = cots[k] + through[k : k + 1] * cots[k + 1]

    last = lax.broadcasted_iota(jnp.int32, (1, CHUNK), 1) == CHUNK - 1
    for k in range(DEPTH):
        at = lanes(k)
        span = pl.ds(k * CHUNK, CHUNK)
        signal, grad, pre = x_s[0, :, span], x_s[1, :, span], pre_s[:, span]
        b, c = coeffs(k, 0), coeffs(k, 1)
        step = dt[k : k + 1]
        rise, fall = from_start[k : k + 1], to_end[k : k + 1]
        signal32, grad32 = signal.astype(F32), grad.astype(F32)
        stepped32 = signal32 * step
        stepped = stepped32.astype(BF16)
        carried = (stepped32 * fall).astype(BF16)
        arrived = (grad32 * rise).astype(BF16)
        state, cot = states[k].astype(BF16), cots[k + 1].astype(BF16)
        decay = jnp.where(
            upper, jnp.exp(jnp.minimum(run[k : k + 1] - run_t[:, k : k + 1], 0.0)), 0.0
        )
        mixing = (dot(b, c, NT) * decay).astype(BF16)
        out = dot(stepped, mixing) + dot(state, c, NT) * rise
        back = dot(grad, mixing, NT) + dot(cot, b, NT) * fall
        pair = (dot(stepped, grad, TN) * decay).astype(BF16)
        b_grad = dot(pair, c) + dot(carried, cot, TN)
        c_grad = dot(pair, b, TN) + dot(arrived, state, TN)
        sig = 1.0 / (1.0 + jnp.exp(-pre))
        pre_grad = (back * step) * (sig * (1.0 + pre * (1.0 - sig)))
        for which, value in enumerate((pre_grad, out)):
            left, right = value[:, :BLOCK], value[:, BLOCK:]
            own_mine[which, :, at] = jnp.where(even, left, right).astype(BF16)
            own_theirs[which, :, at] = jnp.where(even, right, left).astype(BF16)
        low = jnp.concatenate([b_grad[:, :BLOCK], c_grad[:, :BLOCK]], axis=1)
        high = jnp.concatenate([b_grad[:, BLOCK:], c_grad[:, BLOCK:]], axis=1)
        for h in range(2):
            rows_h = slice(h * BLOCK, (h + 1) * BLOCK)
            mine_ref[2 * k + h, :BLOCK, :] = jnp.where(even, low[rows_h], high[rows_h]).astype(BF16)
            theirs_ref[2 * k + h, :BLOCK, :] = jnp.where(
                even, high[rows_h], low[rows_h]
            ).astype(BF16)
        step_grad = jnp.sum(signal32 * back, axis=0, keepdims=True)
        steps[k : k + 1, :] = step_grad
        anchor = jnp.sum(states[k + 1] * cots[k + 1])
        turned = jnp.sum(grad32 * out, axis=0, keepdims=True) - step * step_grad
        weigh[k : k + 1, :] = turned + jnp.where(last, anchor, 0.0)
    decays = dot(weigh[...], (rows >= cols).astype(F32), precision=HIGH)
    blank = jnp.zeros((16, STATE), F32)
    which_row = lax.broadcasted_iota(jnp.int32, (16, STATE), 0)
    for k in range(DEPTH):
        for h in range(2):
            span = slice(h * BLOCK, (h + 1) * BLOCK)
            line = jnp.concatenate([steps[k : k + 1, span], decays[k : k + 1, span]], axis=1)
            coarse = line.astype(BF16).astype(F32)
            tile = jnp.where(which_row == 0, coarse, jnp.where(which_row == 1, line - coarse, 0.0))
            mine_ref[2 * k + h, BLOCK:, :] = tile.astype(BF16)
            theirs_ref[2 * k + h, BLOCK:, :] = blank.astype(BF16)


def run_scan(place, sums, coeffs, start, final):
    tokens = DEPTH * CHUNK
    half = jax.ShapeDtypeStruct((2, HEAD_DIM, tokens // 2), BF16)
    grads = jax.ShapeDtypeStruct((16, BLOCK + 16, STATE), BF16)
    return pl.pallas_call(
        scan_kernel,
        out_shape=[half, half, grads, grads],
        in_specs=[SM] + [VM] * 9,
        out_specs=[VM] * 4,
        scratch_shapes=[
            pltpu.VMEM((2, HEAD_DIM, tokens), BF16),
            pltpu.VMEM((HEAD_DIM, tokens), F32),
            pltpu.VMEM((DEPTH + 1, HEAD_DIM, STATE), F32),
            pltpu.VMEM((DEPTH + 1, HEAD_DIM, STATE), F32),
            pltpu.VMEM((DEPTH, CHUNK), F32),
            pltpu.VMEM((DEPTH, CHUNK), F32),
            pltpu.VMEM((2, DEPTH, CHUNK), F32),
        ],
        compiler_params=ROOM,
        cost_estimate=pl.CostEstimate(
            flops=2_000_000_000, bytes_accessed=10_000_000, transcendentals=1_000_000
        ),
    )(place, *sums, coeffs, start, final)


def body(
    layer_input,
    output_grad,
    inproj_weight,
    outproj_weight,
    input_coeffs,
    output_coeffs,
    step_sizes,
    log_decay,
    state_start,
    state_grad,
):
    row = lax.axis_index("row")
    column = lax.axis_index("col")
    x, y = row // SIDE, row % SIDE
    z, core = column // 2, column % 2
    place = jnp.stack([z, core, x, y]).astype(jnp.int32)
    group = z * STATE
    rates = jnp.concatenate([step_sizes, log_decay], axis=0).reshape(8, 2 * STATE)
    coarse = lax.reduce_precision(rates, 8, 7)
    coeffs = jnp.concatenate(
        [
            jnp.concatenate(
                [
                    lax.dynamic_slice_in_dim(input_coeffs, group, STATE, 1),
                    lax.dynamic_slice_in_dim(output_coeffs, group, STATE, 1),
                ],
                axis=1,
            ),
            coarse.astype(BF16),
            (rates - coarse).astype(BF16),
        ],
        axis=0,
    )
    own_coeffs = coeffs
    coeffs = lax.all_gather(coeffs, "row", axis=0, tiled=True).reshape(16, BLOCK + 16, 2 * STATE)
    start = lax.dynamic_index_in_dim(state_start, row, 0, False)
    final = lax.dynamic_index_in_dim(state_grad, row, 0, False)
    in_w = inproj_weight.T

    packed_mine = pack(gather_z(layer_input), gather_z(output_grad), own_coeffs)
    packed_theirs = swap_core(packed_mine)
    units = [
        project(place, packed_mine, in_w, outproj_weight, True),
        project(place, packed_theirs, in_w, outproj_weight, False),
    ]
    units = reduce_pair(units, (shift_y, shift_x), coeffs)
    sums_mine, sums_theirs = reduce_small(units, (shift_x, shift_y))

    own_mine, own_theirs, mine, theirs = run_scan(
        place, [*sums_mine, *sums_theirs], coeffs, start, final
    )
    pieces_mine, pieces_theirs = gather_small((own_mine, own_theirs), (shift_y, shift_x))
    units = (
        line_up(place, pieces_mine, 3, *pieces_theirs[2:4]),
        line_up(place, pieces_theirs, 2, *pieces_mine[2:4]),
    )
    pieces_mine, pieces_theirs = gather_pair(units, (shift_x, shift_y))
    both = bump(mine, swap_core(theirs), 0, pieces_mine[6])
    both = lax.all_to_all(both, "row", 0, 0)
    pg_theirs, so_theirs, update_theirs = run_update(place, pieces_theirs, in_w, False)
    pg_mine, so_mine, update_mine = run_update(place, pieces_mine, in_w, True, update_theirs)
    update_theirs = swap_core(update_theirs)
    input_grad, first, second = scatter_z(add(update_mine, update_theirs).astype(BF16), both)
    inproj_grad = weight_grad(pg_mine, packed_mine, pg_theirs, packed_theirs, 0, first)
    outproj_grad = weight_grad(so_mine, packed_mine, so_theirs, packed_theirs, 1, second)

    coeff_grads = jnp.sum(both[:, :BLOCK].astype(F32), axis=0)
    lines = add(both[:, BLOCK], both[:, BLOCK + 1])
    return (
        input_grad,
        inproj_grad,
        outproj_grad,
        coeff_grads[:, :BLOCK],
        coeff_grads[:, BLOCK:],
        lines[:, :BLOCK],
        lines[:, BLOCK:],
    )


def solution(mesh):
    return jax.shard_map(
        body,
        mesh=mesh,
        in_specs=(
            P("col", "row"),
            P("col", "row"),
            P("row", "col"),
            P("col", "row"),
            P("row", None),
            P("row", None),
            P("col", "row"),
            P("col", "row"),
            P("col", None, None),
            P("col", None, None),
        ),
        out_specs=(
            P("col", "row"),
            P("row", "col"),
            P("col", "row"),
            P("row", "col"),
            P("row", "col"),
            P("col", "row"),
            P("col", "row"),
        ),
        check_vma=False,
    )
```

```python
import functools

import jax
import jax.numpy as jnp
from jax import lax
from jax.experimental import pallas as pl
from jax.experimental.pallas import tpu as pltpu
from jax.sharding import PartitionSpec as P

HEAD_DIM = 64
STATE = 256
SIDE = 4
DEPTH = 8
BLOCK = 128
CHUNK = 256
F32 = jnp.float32
BF16 = jnp.bfloat16
VM = pl.BlockSpec(memory_space=pltpu.VMEM)
SM = pl.BlockSpec(memory_space=pltpu.SMEM)
ANY = pl.BlockSpec(memory_space=pl.ANY)
ROOM = pltpu.CompilerParams(vmem_limit_bytes=12 * 1024 * 1024)
SMALL = pltpu.CompilerParams(vmem_limit_bytes=6 * 1024 * 1024)


def shift_y(a, d):
    pairs = [(x * 4 + y, x * 4 + (y + d) % 4) for x in range(4) for y in range(4)]
    return lax.ppermute(a, "row", pairs)


def shift_x(a, d):
    pairs = [(x * 4 + y, (x + d) % 4 * 4 + y) for x in range(4) for y in range(4)]
    return lax.ppermute(a, "row", pairs)


def shift_z(a, d):
    pairs = [(z * 2 + c, (z + d) % 8 * 2 + c) for z in range(8) for c in range(2)]
    return lax.ppermute(a, "col", pairs)


def swap_core(a):
    return lax.ppermute(a, "col", [(i, i ^ 1) for i in range(16)])


def add(*terms):
    total = terms[0].astype(F32)
    for term in terms[1:]:
        total = total + term.astype(F32)
    return total


def gather_z(own, *waits):
    up1, down1 = shift_z(own, 1), shift_z(own, -1)
    up2, down2 = shift_z(up1, 1), shift_z(down1, -1)
    up3, down3 = shift_z(up2, 1), shift_z(down2, -1)
    far = (shift_z(cut(up3, 0, *waits), 1), shift_z(cut(down3, 1), -1))
    return [own, down1, down2, down3, *far, up3, up2, up1]


def bump_kernel(first, base, extra, *refs):
    out = refs[-1]
    if extra.shape == base.shape:
        out[...] = add(base[...], extra[...]).astype(BF16)
    else:
        out[...] = base[...]
        at = pl.ds(first, extra.shape[0])
        out[at] = add(base[at], extra[...]).astype(BF16)


def bump(base, extra, first, *waits):
    return pl.pallas_call(
        functools.partial(bump_kernel, first),
        out_shape=jax.ShapeDtypeStruct(base.shape, BF16),
        in_specs=[VM, VM] + [ANY] * len(waits),
        out_specs=VM,
        compiler_params=SMALL,
    )(base, extra, *waits)


def own_kernel(c0, first_up, second_up, first_down, second_down, *refs):
    outs = refs[-5:]
    half = first_up.shape[0]
    near = add(c0[:half], first_up[...], first_down[...]).astype(BF16)
    away = add(c0[half:], second_up[...], second_down[...]).astype(BF16)
    outs[0][...] = near[0]
    outs[1][...] = near[1]
    outs[2][...] = away[0, :1]
    outs[3][...] = away[0, 1:]
    outs[4][...] = away[1]


def own_sum(c0, pieces, *waits):
    whole = jax.ShapeDtypeStruct(c0.shape[1:], BF16)
    half = jax.ShapeDtypeStruct((1, *c0.shape[2:]), BF16)
    return pl.pallas_call(
        own_kernel,
        out_shape=[whole, whole, half, half, whole],
        in_specs=[VM] * 5 + [ANY] * len(waits),
        out_specs=[VM] * 5,
        compiler_params=SMALL,
    )(c0, *pieces, *waits)


def reduce_pair(units, shifts, *waits):
    far, free = [], []
    for (c0, c1a, c1b, c2a, c2b, c3a, c3b), shift in zip(units, shifts):
        far.append((shift(c2a, 1), shift(c2b, -1)))
        free.append((shift(c1b, 1), shift(c3a, -1)))
    sums = []
    for i, shift in enumerate(shifts):
        c0, c1a, c1b, c2a, c2b, c3a, c3b = units[i]
        other = far[1 - i]
        last_up = shift(bump(c1a, far[i][0], 0, *other), 1)
        last_down = shift(bump(c3b, far[i][1], 0, *other), -1)
        sums.append((c0, (last_up, free[i][0], free[i][1], last_down)))
    return [own_sum(c0, pieces, *waits) for c0, pieces in sums]


def reduce_small(units, shifts):
    far = [
        (shift(c2a, 1), shift(c2b, -1))
        for (c0, c1, c2a, c2b, c3), shift in zip(units, shifts)
    ]
    parts = []
    for i, shift in enumerate(shifts):
        c0, c1, c2a, c2b, c3 = units[i]
        other = far[1 - i]
        up = shift(bump(c1, far[i][0], 0, *other), 1)
        down = shift(bump(c3, far[i][1], 1, *other), -1)
        parts.append((c0, up, down))
    return parts


def cut_kernel(first, base, *refs):
    out = refs[-1]
    out[...] = base[pl.ds(first, out.shape[0])]


def cut(base, first, *waits):
    half = base.shape[0] // 2
    return pl.pallas_call(
        functools.partial(cut_kernel, first * half),
        out_shape=jax.ShapeDtypeStruct((half, *base.shape[1:]), BF16),
        in_specs=[VM] + [ANY] * len(waits),
        out_specs=VM,
        compiler_params=SMALL,
    )(base, *waits)


def gather_small(units, shifts):
    near = [(shift(own, 1), shift(own, -1)) for own, shift in zip(units, shifts)]
    lines = []
    for i, shift in enumerate(shifts):
        (up, down), other = near[i], near[1 - i]
        far = shift(cut(up, 0, *other), 1), shift(cut(down, 1, *other), -1)
        lines.append((units[i], down, *far, up))
    return lines


def gather_pair(units, shifts):
    first = [(shift(lo, 1), shift(hi, -1)) for (lo, hi), shift in zip(units, shifts)]
    rest = [(shift(hi, 1), shift(lo, -1)) for (lo, hi), shift in zip(units, shifts)]
    far = [(shift(up, 1), shift(down, -1)) for (up, down), shift in zip(first, shifts)]
    return [
        (lo, hi, down_lo, down_hi, far_lo, far_hi, up_lo, up_hi)
        for (lo, hi), (up_lo, down_hi), (up_hi, down_lo), (far_lo, far_hi) in zip(
            units, first, rest, far
        )
    ]


def scatter_z(total, beside, last):
    rows = total.shape[0] // DEPTH
    half = rows // 2
    chunks = [total[d * rows : (d + 1) * rows] for d in range(DEPTH)]
    up, down = shift_z(cut(chunks[4], 0), 1), shift_z(cut(chunks[4], 1), -1)
    done = beside(0, total)
    up, down = bump(chunks[3], up, 0, done), bump(chunks[5], down, half)
    done = beside(1, up)
    up, down = shift_z(up, 1), shift_z(down, -1)
    up, down = bump(chunks[2], up, 0, done), bump(chunks[6], down, 0)
    done = beside(2, up)
    up, down = shift_z(up, 1), shift_z(down, -1)
    up, down = bump(chunks[1], up, 0, done, last), bump(chunks[7], down, 0)
    beside(3, up)
    up, down = shift_z(up, 1), shift_z(down, -1)
    return add(chunks[0], up, down).astype(BF16)


def dot(a, b, dims=((1,), (0,)), precision=None):
    return lax.dot_general(a, b, (dims, ((), ())), preferred_element_type=F32, precision=precision)


NT = ((1,), (1,))
TN = ((0,), (0,))
HIGH = lax.Precision.HIGHEST


def turn(at, d):
    return lax.rem(at + d, SIDE)


def pack_kernel(*refs):
    out = refs[-1]
    pieces = refs[:18]
    for which in range(2):
        row = 0
        for piece in pieces[which * 9 : which * 9 + 9]:
            out[which, row : row + piece.shape[0], :] = piece[...]
            row += piece.shape[0]


def pack(inputs, grads, *waits):
    shape = (2, DEPTH * BLOCK, inputs[0].shape[1])
    return pl.pallas_call(
        pack_kernel,
        out_shape=jax.ShapeDtypeStruct(shape, BF16),
        in_specs=[VM] * 18 + [ANY] * len(waits),
        out_specs=VM,
        compiler_params=SMALL,
    )(*inputs, *grads, *waits)


def project_kernel(y_first, place, tokens_ref, in_w, grad_w, c0, c1a, c1b, c2a, c2b, c3a, c3b):
    x, y = place[2], place[3]
    halves = ((c0, c0), (c1a, c1b), (c2a, c2b), (c3a, c3b))

    def one(tile, carry):
        span = pl.ds(pl.multiple_of(tile * CHUNK, CHUNK), CHUNK)
        for which, w_ref in enumerate((in_w, grad_w)):
            tokens = tokens_ref[which, span, :]
            for d in range(SIDE):
                pieces = []
                for i in range(SIDE):
                    at_x, at_y = (turn(x, i), turn(y, d)) if y_first else (turn(x, d), turn(y, i))
                    start = pl.multiple_of((at_x * SIDE + at_y) * HEAD_DIM, HEAD_DIM)
                    pieces.append(w_ref[pl.ds(start, HEAD_DIM), :])
                part = dot(jnp.concatenate(pieces, axis=0), tokens, NT).astype(BF16)
                for i in range(SIDE):
                    rows = part[i * HEAD_DIM : (i + 1) * HEAD_DIM]
                    halves[d][i // 2][i if d == 0 else i % 2, which, :, span] = rows
        return carry

    lax.fori_loop(0, DEPTH * BLOCK // CHUNK, one, 0)


def project(place, tokens, in_w, grad_w, y_first):
    count, width = tokens.shape[1:]
    chunk = jax.ShapeDtypeStruct((SIDE, 2, HEAD_DIM, count), BF16)
    half = jax.ShapeDtypeStruct((SIDE // 2, 2, HEAD_DIM, count), BF16)
    return pl.pallas_call(
        functools.partial(project_kernel, y_first),
        out_shape=[chunk] + [half] * 6,
        in_specs=[SM] + [VM] * 3,
        out_specs=[VM] * 7,
        compiler_params=SMALL,
        cost_estimate=pl.CostEstimate(
            flops=4 * 1024 * count * width, bytes_accessed=10_000_000, transcendentals=0
        ),
    )(place, tokens, in_w, grad_w)


def line_kernel(axis, place, own, down, far_a, far_b, up, *refs):
    outs = refs[-2:]
    at = place[axis]
    for slot in range(SIDE):
        d = lax.rem(slot - at + SIDE, SIDE)
        target = outs[slot // 2].at[slot % 2]
        far = jnp.concatenate([far_a[...], far_b[...]], axis=0)
        near = jnp.where(d == 0, own[...], down[...])
        away = jnp.where(d == 2, far, up[...])
        target[...] = jnp.where(d < 2, near, away)


def line_up(place, pieces, axis, *waits):
    half = jax.ShapeDtypeStruct((SIDE // 2, *pieces[0].shape), BF16)
    return pl.pallas_call(
        functools.partial(line_kernel, axis),
        out_shape=[half, half],
        in_specs=[SM] + [VM] * 5 + [ANY] * len(waits),
        out_specs=[VM] * 2,
        compiler_params=SMALL,
    )(place, *pieces, *waits)


def update_kernel(y_first, place, *refs):
    x, y = place[2], place[3]
    w_ref, (grads, outs, update) = refs[8], refs[-3:]
    for n, ref in enumerate(refs[:8]):
        d = n // 2
        for i in range(2):
            slot = n % 2 * 2 + i
            at_x, at_y = (turn(x, d), slot) if y_first else (slot, turn(y, d))
            start = pl.multiple_of((at_x * SIDE + at_y) * HEAD_DIM, HEAD_DIM)
            grads[pl.ds(start, HEAD_DIM), :] = ref[i, 0]
            outs[pl.ds(start, HEAD_DIM), :] = ref[i, 1]
    for tile in range(DEPTH * BLOCK // CHUNK):
        span = pl.ds(tile * CHUNK, CHUNK)
        update[span, :] = dot(grads[:, span], w_ref[...], TN).astype(BF16)


def run_update(place, pieces, w, y_first, *waits):
    tokens = pieces[0].shape[-1]
    whole = jax.ShapeDtypeStruct((w.shape[0], tokens), BF16)
    return pl.pallas_call(
        functools.partial(update_kernel, y_first),
        out_shape=[whole, whole, jax.ShapeDtypeStruct((tokens, w.shape[1]), BF16)],
        in_specs=[SM] + [VM] * 9 + [ANY] * len(waits),
        out_specs=[VM] * 3,
        compiler_params=ROOM,
        cost_estimate=pl.CostEstimate(
            flops=2 * w.size * tokens, bytes_accessed=6_000_000, transcendentals=0
        ),
    )(place, *pieces, w, *waits)


def weight_kernel(which, part, a_mine, b_mine, a_theirs, b_theirs, *refs):
    out = refs[-1]
    tiles = a_mine.shape[0] // CHUNK // 2
    if part == 1:
        before = refs[1]
        if which == 0:
            out[:, : tiles * CHUNK] = before[:, : tiles * CHUNK]
        else:
            out[: tiles * CHUNK, :] = before[: tiles * CHUNK, :]
    for tile in range(part * tiles, part * tiles + tiles):
        span = pl.ds(tile * CHUNK, CHUNK)
        value = dot(a_mine[span, :], b_mine[which]) + dot(a_theirs[span, :], b_theirs[which])
        if which == 0:
            out[:, span] = value.T
        else:
            out[span, :] = value


def weight_grad(operands, which, part, before, wait):
    rows, cols = operands[0].shape[0], operands[1].shape[2]
    again = [] if before is None else [before]
    return pl.pallas_call(
        functools.partial(weight_kernel, which, part),
        out_shape=jax.ShapeDtypeStruct((rows, cols) if which else (cols, rows), F32),
        in_specs=[VM] * 4 + [ANY] + [VM] * len(again),
        out_specs=VM,
        compiler_params=ROOM,
        cost_estimate=pl.CostEstimate(
            flops=2 * rows * cols * 1024, bytes_accessed=4_000_000, transcendentals=0
        ),
    )(*operands, wait, *again)


def scan_kernel(place, *refs):
    sums = refs[:6]
    coeff_ref, start_ref, final_ref = refs[6:9]
    own_mine, own_theirs, mine_ref, theirs_ref = refs[9:13]
    x_s, pre_s, states, cots, weigh, steps, rates = refs[13:]
    z, core = place[0], place[1]
    even = core == 0

    def lanes(k):
        return pl.ds(pl.multiple_of(lax.rem(k - z + DEPTH, DEPTH) * BLOCK, BLOCK), BLOCK)

    def summed(unit, which, at):
        return add(*(ref[which, :, at] for ref in sums[unit * 3 : unit * 3 + 3]))

    def ordered(mine, theirs):
        return jnp.concatenate(
            [jnp.where(even, mine, theirs), jnp.where(even, theirs, mine)], axis=1
        )

    def coeffs(k, which):
        block = coeff_ref[2 * k : 2 * k + 2, :BLOCK, which * STATE : (which + 1) * STATE]
        return block.reshape(CHUNK, STATE)

    rows = lax.broadcasted_iota(jnp.int32, (CHUNK, CHUNK), 0)
    cols = lax.broadcasted_iota(jnp.int32, (CHUNK, CHUNK), 1)
    upper = rows <= cols
    x, y = place[2], place[3]
    packed_row = lax.broadcasted_iota(jnp.int32, (16, BLOCK), 0)
    for r in range(16):
        tile = coeff_ref[r, BLOCK:, pl.ds(pl.multiple_of(y * BLOCK, BLOCK), BLOCK)].astype(F32)
        for which in range(2):
            chosen = lax.rem(packed_row, 8) == x + 4 * which
            line = jnp.sum(jnp.where(chosen, tile, 0.0), axis=0, keepdims=True)
            rates[which, r // 2 : r // 2 + 1, r % 2 * BLOCK : (r % 2 + 1) * BLOCK] = line
    dt = rates[0]
    run = dot(rates[1], upper.astype(F32), precision=HIGH)
    closing = run[:, CHUNK - 1 :]
    from_start = jnp.exp(run)
    to_end = jnp.exp(closing - run)
    through = jnp.exp(closing)
    run_t = run.T

    for k in range(DEPTH):
        at = lanes(k)
        span = pl.ds(k * CHUNK, CHUNK)
        pre = ordered(summed(0, 0, at), summed(1, 0, at))
        grad = ordered(summed(0, 1, at), summed(1, 1, at)).astype(BF16)
        pre_s[:, span] = pre
        signal = (pre / (1.0 + jnp.exp(-pre))).astype(BF16)
        x_s[0, :, span] = signal
        x_s[1, :, span] = grad
        carried = (signal.astype(F32) * (dt[k : k + 1] * to_end[k : k + 1])).astype(BF16)
        states[k + 1] = dot(carried, coeffs(k, 0))
        arrived = (grad.astype(F32) * from_start[k : k + 1]).astype(BF16)
        cots[k] = dot(arrived, coeffs(k, 1))
    states[0] = start_ref[...]
    cots[DEPTH] = final_ref[...]
    for k in range(DEPTH):
        states[k + 1] = states[k + 1] + through[k : k + 1] * states[k]
    for k in reversed(range(DEPTH)):
        cots[k] = cots[k] + through[k : k + 1] * cots[k + 1]

    last = lax.broadcasted_iota(jnp.int32, (1, CHUNK), 1) == CHUNK - 1
    for k in range(DEPTH):
        at = lanes(k)
        span = pl.ds(k * CHUNK, CHUNK)
        signal, grad, pre = x_s[0, :, span], x_s[1, :, span], pre_s[:, span]
        b, c = coeffs(k, 0), coeffs(k, 1)
        step = dt[k : k + 1]
        rise, fall = from_start[k : k + 1], to_end[k : k + 1]
        signal32, grad32 = signal.astype(F32), grad.astype(F32)
        stepped32 = signal32 * step
        stepped = stepped32.astype(BF16)
        carried = (stepped32 * fall).astype(BF16)
        arrived = (grad32 * rise).astype(BF16)
        state, cot = states[k].astype(BF16), cots[k + 1].astype(BF16)
        decay = jnp.where(
            upper, jnp.exp(jnp.minimum(run[k : k + 1] - run_t[:, k : k + 1], 0.0)), 0.0
        )
        mixing = (dot(b, c, NT) * decay).astype(BF16)
        out = dot(stepped, mixing) + dot(state, c, NT) * rise
        back = dot(grad, mixing, NT) + dot(cot, b, NT) * fall
        pair = (dot(stepped, grad, TN) * decay).astype(BF16)
        b_grad = dot(pair, c) + dot(carried, cot, TN)
        c_grad = dot(pair, b, TN) + dot(arrived, state, TN)
        sig = 1.0 / (1.0 + jnp.exp(-pre))
        pre_grad = (back * step) * (sig * (1.0 + pre * (1.0 - sig)))
        for which, value in enumerate((pre_grad, out)):
            left, right = value[:, :BLOCK], value[:, BLOCK:]
            own_mine[which, :, at] = jnp.where(even, left, right).astype(BF16)
            own_theirs[which, :, at] = jnp.where(even, right, left).astype(BF16)
        low = jnp.concatenate([b_grad[:, :BLOCK], c_grad[:, :BLOCK]], axis=1)
        high = jnp.concatenate([b_grad[:, BLOCK:], c_grad[:, BLOCK:]], axis=1)
        for h in range(2):
            rows_h = slice(h * BLOCK, (h + 1) * BLOCK)
            mine_ref[2 * k + h, :BLOCK, :] = jnp.where(even, low[rows_h], high[rows_h]).astype(BF16)
            theirs_ref[2 * k + h, :BLOCK, :] = jnp.where(
                even, high[rows_h], low[rows_h]
            ).astype(BF16)
        step_grad = jnp.sum(signal32 * back, axis=0, keepdims=True)
        steps[k : k + 1, :] = step_grad
        anchor = jnp.sum(states[k + 1] * cots[k + 1])
        turned = jnp.sum(grad32 * out, axis=0, keepdims=True) - step * step_grad
        weigh[k : k + 1, :] = turned + jnp.where(last, anchor, 0.0)
    decays = dot(weigh[...], (rows >= cols).astype(F32), precision=HIGH)
    blank = jnp.zeros((16, STATE), F32)
    which_row = lax.broadcasted_iota(jnp.int32, (16, STATE), 0)
    for k in range(DEPTH):
        for h in range(2):
            span = slice(h * BLOCK, (h + 1) * BLOCK)
            line = jnp.concatenate([steps[k : k + 1, span], decays[k : k + 1, span]], axis=1)
            coarse = line.astype(BF16).astype(F32)
            tile = jnp.where(which_row == 0, coarse, jnp.where(which_row == 1, line - coarse, 0.0))
            mine_ref[2 * k + h, BLOCK:, :] = tile.astype(BF16)
            theirs_ref[2 * k + h, BLOCK:, :] = blank.astype(BF16)


def run_scan(place, sums, coeffs, start, final):
    tokens = DEPTH * CHUNK
    half = jax.ShapeDtypeStruct((2, HEAD_DIM, tokens // 2), BF16)
    grads = jax.ShapeDtypeStruct((16, BLOCK + 16, STATE), BF16)
    return pl.pallas_call(
        scan_kernel,
        out_shape=[half, half, grads, grads],
        in_specs=[SM] + [VM] * 9,
        out_specs=[VM] * 4,
        scratch_shapes=[
            pltpu.VMEM((2, HEAD_DIM, tokens), BF16),
            pltpu.VMEM((HEAD_DIM, tokens), F32),
            pltpu.VMEM((DEPTH + 1, HEAD_DIM, STATE), F32),
            pltpu.VMEM((DEPTH + 1, HEAD_DIM, STATE), F32),
            pltpu.VMEM((DEPTH, CHUNK), F32),
            pltpu.VMEM((DEPTH, CHUNK), F32),
            pltpu.VMEM((2, DEPTH, CHUNK), F32),
        ],
        compiler_params=ROOM,
        cost_estimate=pl.CostEstimate(
            flops=2_000_000_000, bytes_accessed=10_000_000, transcendentals=1_000_000
        ),
    )(place, *sums, coeffs, start, final)


def body(
    layer_input,
    output_grad,
    inproj_weight,
    outproj_weight,
    input_coeffs,
    output_coeffs,
    step_sizes,
    log_decay,
    state_start,
    state_grad,
):
    row = lax.axis_index("row")
    column = lax.axis_index("col")
    x, y = row // SIDE, row % SIDE
    z, core = column // 2, column % 2
    place = jnp.stack([z, core, x, y]).astype(jnp.int32)
    group = z * STATE
    rates = jnp.concatenate([step_sizes, log_decay], axis=0).reshape(8, 2 * STATE)
    coarse = lax.reduce_precision(rates, 8, 7)
    coeffs = jnp.concatenate(
        [
            jnp.concatenate(
                [
                    lax.dynamic_slice_in_dim(input_coeffs, group, STATE, 1),
                    lax.dynamic_slice_in_dim(output_coeffs, group, STATE, 1),
                ],
                axis=1,
            ),
            coarse.astype(BF16),
            (rates - coarse).astype(BF16),
        ],
        axis=0,
    )
    own_coeffs = coeffs
    coeffs = lax.all_gather(coeffs, "row", axis=0, tiled=True).reshape(16, BLOCK + 16, 2 * STATE)
    start = lax.dynamic_index_in_dim(state_start, row, 0, False)
    final = lax.dynamic_index_in_dim(state_grad, row, 0, False)
    in_w = inproj_weight.T

    packed_mine = pack(gather_z(layer_input, own_coeffs), gather_z(output_grad, in_w))
    packed_theirs = swap_core(packed_mine)
    units = [
        project(place, packed_mine, in_w, outproj_weight, True),
        project(place, packed_theirs, in_w, outproj_weight, False),
    ]
    units = reduce_pair(units, (shift_y, shift_x))
    sums_mine, sums_theirs = reduce_small(units, (shift_x, shift_y))

    own_mine, own_theirs, mine, theirs = run_scan(
        place, [*sums_mine, *sums_theirs], coeffs, start, final
    )
    pieces_mine, pieces_theirs = gather_small((own_mine, own_theirs), (shift_y, shift_x))
    swapped = swap_core(theirs)
    units = (
        line_up(place, pieces_mine, 3, *pieces_theirs[2:4], swapped),
        line_up(place, pieces_theirs, 2, *pieces_mine[2:4], swapped),
    )
    pieces_mine, pieces_theirs = gather_pair(units, (shift_x, shift_y))
    pg_theirs, so_theirs, update_theirs = run_update(place, pieces_theirs, in_w, False)
    pg_mine, so_mine, update_mine = run_update(place, pieces_mine, in_w, True, update_theirs)
    both = bump(mine, swapped, 0, update_theirs)
    both = lax.all_to_all(both, "row", 0, 0)
    update_theirs = swap_core(update_theirs)
    operands = (
        (pg_mine, packed_mine, pg_theirs, packed_theirs),
        (so_mine, packed_mine, so_theirs, packed_theirs),
    )
    grads = [None, None]

    def beside(i, value):
        which = i // 2
        grads[which] = weight_grad(operands[which], which, i % 2, grads[which], value)
        return grads[which]

    input_grad = scatter_z(add(update_mine, update_theirs).astype(BF16), beside, both)
    inproj_grad, outproj_grad = grads

    coeff_grads = jnp.sum(both[:, :BLOCK].astype(F32), axis=0)
    lines = add(both[:, BLOCK], both[:, BLOCK + 1])
    return (
        input_grad,
        inproj_grad,
        outproj_grad,
        coeff_grads[:, :BLOCK],
        coeff_grads[:, BLOCK:],
        lines[:, :BLOCK],
        lines[:, BLOCK:],
    )


def solution(mesh):
    return jax.shard_map(
        body,
        mesh=mesh,
        in_specs=(
            P("col", "row"),
            P("col", "row"),
            P("row", "col"),
            P("col", "row"),
            P("row", None),
            P("row", None),
            P("col", "row"),
            P("col", "row"),
            P("col", None, None),
            P("col", None, None),
        ),
        out_specs=(
            P("col", "row"),
            P("row", "col"),
            P("col", "row"),
            P("row", "col"),
            P("row", "col"),
            P("col", "row"),
            P("col", "row"),
        ),
        check_vma=False,
    )
```

```python
import functools

import jax
import jax.numpy as jnp
from jax import lax
from jax.experimental import pallas as pl
from jax.experimental.pallas import tpu as pltpu
from jax.sharding import PartitionSpec as P

HEAD_DIM = 64
STATE = 256
SIDE = 4
DEPTH = 8
BLOCK = 128
CHUNK = 256
F32 = jnp.float32
BF16 = jnp.bfloat16
VM = pl.BlockSpec(memory_space=pltpu.VMEM)
SM = pl.BlockSpec(memory_space=pltpu.SMEM)
ANY = pl.BlockSpec(memory_space=pl.ANY)
ROOM = pltpu.CompilerParams(vmem_limit_bytes=40 * 1024 * 1024)
SMALL = pltpu.CompilerParams(vmem_limit_bytes=6 * 1024 * 1024)


def shift_y(a, d):
    pairs = [(x * 4 + y, x * 4 + (y + d) % 4) for x in range(4) for y in range(4)]
    return lax.ppermute(a, "row", pairs)


def shift_x(a, d):
    pairs = [(x * 4 + y, (x + d) % 4 * 4 + y) for x in range(4) for y in range(4)]
    return lax.ppermute(a, "row", pairs)


def shift_z(a, d):
    pairs = [(z * 2 + c, (z + d) % 8 * 2 + c) for z in range(8) for c in range(2)]
    return lax.ppermute(a, "col", pairs)


def swap_core(a):
    return lax.ppermute(a, "col", [(i, i ^ 1) for i in range(16)])


def add(*terms):
    total = terms[0].astype(F32)
    for term in terms[1:]:
        total = total + term.astype(F32)
    return total


def gather_z(own):
    half = own.shape[0] // 2
    up1, down1 = shift_z(own, 1), shift_z(own, -1)
    up2, down2 = shift_z(up1, 1), shift_z(down1, -1)
    up3, down3 = shift_z(up2, 1), shift_z(down2, -1)
    far = (shift_z(up3[:half], 1), shift_z(down3[half:], -1))
    return [own, down1, down2, down3, *far, up3, up2, up1]


def bump_kernel(first, base, extra, *refs):
    out = refs[-1]
    if extra.shape == base.shape:
        out[...] = add(base[...], extra[...]).astype(BF16)
    else:
        out[...] = base[...]
        at = pl.ds(first, extra.shape[0])
        out[at] = add(base[at], extra[...]).astype(BF16)


def bump(base, extra, first, *waits):
    return pl.pallas_call(
        functools.partial(bump_kernel, first),
        out_shape=jax.ShapeDtypeStruct(base.shape, BF16),
        in_specs=[VM, VM] + [ANY] * len(waits),
        out_specs=VM,
        compiler_params=SMALL,
    )(base, extra, *waits)


def own_kernel(c0, first_up, second_up, first_down, second_down, *refs):
    outs = refs[-5:]
    half = first_up.shape[0]
    near = add(c0[:half], first_up[...], first_down[...]).astype(BF16)
    away = add(c0[half:], second_up[...], second_down[...]).astype(BF16)
    outs[0][...] = near[0]
    outs[1][...] = near[1]
    outs[2][...] = away[0, :1]
    outs[3][...] = away[0, 1:]
    outs[4][...] = away[1]


def own_sum(c0, pieces, *waits):
    whole = jax.ShapeDtypeStruct(c0.shape[1:], BF16)
    half = jax.ShapeDtypeStruct((1, *c0.shape[2:]), BF16)
    return pl.pallas_call(
        own_kernel,
        out_shape=[whole, whole, half, half, whole],
        in_specs=[VM] * 5 + [ANY] * len(waits),
        out_specs=[VM] * 5,
        compiler_params=SMALL,
    )(c0, *pieces, *waits)


def reduce_pair(units, shifts, *waits):
    far, free = [], []
    for (c0, c1a, c1b, c2a, c2b, c3a, c3b), shift in zip(units, shifts):
        far.append((shift(c2a, 1), shift(c2b, -1)))
        free.append((shift(c1b, 1), shift(c3a, -1)))
    sums = []
    for i, shift in enumerate(shifts):
        c0, c1a, c1b, c2a, c2b, c3a, c3b = units[i]
        other = far[1 - i]
        last_up = shift(bump(c1a, far[i][0], 0, *other), 1)
        last_down = shift(bump(c3b, far[i][1], 0, *other), -1)
        sums.append((c0, (last_up, free[i][0], free[i][1], last_down)))
    return [own_sum(c0, pieces, *waits) for c0, pieces in sums]


def reduce_small(units, shifts):
    far = [
        (shift(c2a, 1), shift(c2b, -1))
        for (c0, c1, c2a, c2b, c3), shift in zip(units, shifts)
    ]
    parts = []
    for i, shift in enumerate(shifts):
        c0, c1, c2a, c2b, c3 = units[i]
        other = far[1 - i]
        up = shift(bump(c1, far[i][0], 0, *other), 1)
        down = shift(bump(c3, far[i][1], 1, *other), -1)
        parts.append((c0, up, down))
    return parts


def cut_kernel(first, base, *refs):
    out = refs[-1]
    out[...] = base[pl.ds(first, out.shape[0])]


def cut(base, first, *waits):
    half = base.shape[0] // 2
    return pl.pallas_call(
        functools.partial(cut_kernel, first * half),
        out_shape=jax.ShapeDtypeStruct((half, *base.shape[1:]), BF16),
        in_specs=[VM] + [ANY] * len(waits),
        out_specs=VM,
        compiler_params=SMALL,
    )(base, *waits)


def gather_small(units, shifts):
    near = [(shift(own, 1), shift(own, -1)) for own, shift in zip(units, shifts)]
    lines = []
    for i, shift in enumerate(shifts):
        (up, down), other = near[i], near[1 - i]
        far = shift(cut(up, 0, *other), 1), shift(cut(down, 1, *other), -1)
        lines.append((units[i], down, *far, up))
    return lines


def gather_pair(units, shifts):
    first = [(shift(lo, 1), shift(hi, -1)) for (lo, hi), shift in zip(units, shifts)]
    rest = [(shift(hi, 1), shift(lo, -1)) for (lo, hi), shift in zip(units, shifts)]
    far = [(shift(up, 1), shift(down, -1)) for (up, down), shift in zip(first, shifts)]
    return [
        (lo, hi, down_lo, down_hi, far_lo, far_hi, up_lo, up_hi)
        for (lo, hi), (up_lo, down_hi), (up_hi, down_lo), (far_lo, far_hi) in zip(
            units, first, rest, far
        )
    ]


def scatter_z(total, *waits):
    rows = total.shape[0] // DEPTH
    half = rows // 2
    chunks = [total[d * rows : (d + 1) * rows] for d in range(DEPTH)]
    up = shift_z(chunks[4][:half], 1)
    down = shift_z(chunks[4][half:], -1)
    up = first = bump(chunks[3], up, 0)
    up, down = shift_z(up, 1), shift_z(bump(chunks[5], down, half), -1)
    up = second = bump(chunks[2], up, 0)
    up, down = shift_z(up, 1), shift_z(bump(chunks[6], down, 0), -1)
    up = shift_z(bump(chunks[1], up, 0, *waits), 1)
    down = shift_z(bump(chunks[7], down, 0), -1)
    return add(chunks[0], up, down).astype(BF16), first, second


def dot(a, b, dims=((1,), (0,)), precision=None):
    return lax.dot_general(a, b, (dims, ((), ())), preferred_element_type=F32, precision=precision)


NT = ((1,), (1,))
TN = ((0,), (0,))
HIGH = lax.Precision.HIGHEST


def turn(at, d):
    return lax.rem(at + d, SIDE)


def pack_kernel(*refs):
    out = refs[-1]
    pieces = refs[:18]
    for which in range(2):
        row = 0
        for piece in pieces[which * 9 : which * 9 + 9]:
            out[which, row : row + piece.shape[0], :] = piece[...]
            row += piece.shape[0]


def pack(inputs, grads, *waits):
    shape = (2, DEPTH * BLOCK, inputs[0].shape[1])
    return pl.pallas_call(
        pack_kernel,
        out_shape=jax.ShapeDtypeStruct(shape, BF16),
        in_specs=[VM] * 18 + [ANY] * len(waits),
        out_specs=VM,
        compiler_params=ROOM,
    )(*inputs, *grads, *waits)


def project_kernel(y_first, place, tokens_ref, in_w, grad_w, c0, c1a, c1b, c2a, c2b, c3a, c3b):
    x, y = place[2], place[3]
    halves = ((c0, c0), (c1a, c1b), (c2a, c2b), (c3a, c3b))

    def one(tile, carry):
        span = pl.ds(pl.multiple_of(tile * CHUNK, CHUNK), CHUNK)
        for which, w_ref in enumerate((in_w, grad_w)):
            tokens = tokens_ref[which, span, :]
            for d in range(SIDE):
                pieces = []
                for i in range(SIDE):
                    at_x, at_y = (turn(x, i), turn(y, d)) if y_first else (turn(x, d), turn(y, i))
                    start = pl.multiple_of((at_x * SIDE + at_y) * HEAD_DIM, HEAD_DIM)
                    pieces.append(w_ref[pl.ds(start, HEAD_DIM), :])
                part = dot(jnp.concatenate(pieces, axis=0), tokens, NT).astype(BF16)
                for i in range(SIDE):
                    rows = part[i * HEAD_DIM : (i + 1) * HEAD_DIM]
                    halves[d][i // 2][i if d == 0 else i % 2, which, :, span] = rows
        return carry

    lax.fori_loop(0, DEPTH * BLOCK // CHUNK, one, 0)


def project(place, tokens, in_w, grad_w, y_first):
    count, width = tokens.shape[1:]
    chunk = jax.ShapeDtypeStruct((SIDE, 2, HEAD_DIM, count), BF16)
    half = jax.ShapeDtypeStruct((SIDE // 2, 2, HEAD_DIM, count), BF16)
    return pl.pallas_call(
        functools.partial(project_kernel, y_first),
        out_shape=[chunk] + [half] * 6,
        in_specs=[SM] + [VM] * 3,
        out_specs=[VM] * 7,
        compiler_params=ROOM,
        cost_estimate=pl.CostEstimate(
            flops=4 * 1024 * count * width, bytes_accessed=10_000_000, transcendentals=0
        ),
    )(place, tokens, in_w, grad_w)


def line_kernel(axis, place, own, down, far_a, far_b, up, *refs):
    outs = refs[-2:]
    at = place[axis]
    for slot in range(SIDE):
        d = lax.rem(slot - at + SIDE, SIDE)
        target = outs[slot // 2].at[slot % 2]
        far = jnp.concatenate([far_a[...], far_b[...]], axis=0)
        near = jnp.where(d == 0, own[...], down[...])
        away = jnp.where(d == 2, far, up[...])
        target[...] = jnp.where(d < 2, near, away)


def line_up(place, pieces, axis, *waits):
    half = jax.ShapeDtypeStruct((SIDE // 2, *pieces[0].shape), BF16)
    return pl.pallas_call(
        functools.partial(line_kernel, axis),
        out_shape=[half, half],
        in_specs=[SM] + [VM] * 5 + [ANY] * len(waits),
        out_specs=[VM] * 2,
        compiler_params=SMALL,
    )(place, *pieces, *waits)


def update_kernel(y_first, place, *refs):
    x, y = place[2], place[3]
    w_ref, (grads, outs, update) = refs[8], refs[-3:]
    for n, ref in enumerate(refs[:8]):
        d = n // 2
        for i in range(2):
            slot = n % 2 * 2 + i
            at_x, at_y = (turn(x, d), slot) if y_first else (slot, turn(y, d))
            start = pl.multiple_of((at_x * SIDE + at_y) * HEAD_DIM, HEAD_DIM)
            grads[pl.ds(start, HEAD_DIM), :] = ref[i, 0]
            outs[pl.ds(start, HEAD_DIM), :] = ref[i, 1]
    for tile in range(DEPTH * BLOCK // CHUNK):
        span = pl.ds(tile * CHUNK, CHUNK)
        update[span, :] = dot(grads[:, span], w_ref[...], TN).astype(BF16)


def run_update(place, pieces, w, y_first, *waits):
    tokens = pieces[0].shape[-1]
    whole = jax.ShapeDtypeStruct((w.shape[0], tokens), BF16)
    return pl.pallas_call(
        functools.partial(update_kernel, y_first),
        out_shape=[whole, whole, jax.ShapeDtypeStruct((tokens, w.shape[1]), BF16)],
        in_specs=[SM] + [VM] * 9 + [ANY] * len(waits),
        out_specs=[VM] * 3,
        compiler_params=ROOM,
        cost_estimate=pl.CostEstimate(
            flops=2 * w.size * tokens, bytes_accessed=6_000_000, transcendentals=0
        ),
    )(place, *pieces, w, *waits)


def weight_kernel(which, a_mine, b_mine, a_theirs, b_theirs, *refs):
    out = refs[-1]
    for tile in range(a_mine.shape[0] // CHUNK):
        span = pl.ds(tile * CHUNK, CHUNK)
        part = dot(a_mine[span, :], b_mine[which]) + dot(a_theirs[span, :], b_theirs[which])
        if which == 0:
            out[:, span] = part.T
        else:
            out[span, :] = part


def weight_grad(a_mine, b_mine, a_theirs, b_theirs, which, *waits):
    rows, cols = a_mine.shape[0], b_mine.shape[2]
    return pl.pallas_call(
        functools.partial(weight_kernel, which),
        out_shape=jax.ShapeDtypeStruct((rows, cols) if which else (cols, rows), F32),
        in_specs=[VM] * 4 + [ANY] * len(waits),
        out_specs=VM,
        compiler_params=ROOM,
        cost_estimate=pl.CostEstimate(
            flops=4 * rows * cols * a_mine.shape[1], bytes_accessed=8_000_000, transcendentals=0
        ),
    )(a_mine, b_mine, a_theirs, b_theirs, *waits)


def scan_kernel(place, *refs):
    sums = refs[:6]
    coeff_ref, start_ref, final_ref = refs[6:9]
    own_mine, own_theirs, mine_ref, theirs_ref = refs[9:13]
    x_s, pre_s, states, cots, weigh, steps, rates = refs[13:]
    z, core = place[0], place[1]
    even = core == 0

    def lanes(k):
        return pl.ds(pl.multiple_of(lax.rem(k - z + DEPTH, DEPTH) * BLOCK, BLOCK), BLOCK)

    def summed(unit, which, at):
        return add(*(ref[which, :, at] for ref in sums[unit * 3 : unit * 3 + 3]))

    def ordered(mine, theirs):
        return jnp.concatenate(
            [jnp.where(even, mine, theirs), jnp.where(even, theirs, mine)], axis=1
        )

    def coeffs(k, which):
        block = coeff_ref[2 * k : 2 * k + 2, :BLOCK, which * STATE : (which + 1) * STATE]
        return block.reshape(CHUNK, STATE)

    rows = lax.broadcasted_iota(jnp.int32, (CHUNK, CHUNK), 0)
    cols = lax.broadcasted_iota(jnp.int32, (CHUNK, CHUNK), 1)
    upper = rows <= cols
    x, y = place[2], place[3]
    packed_row = lax.broadcasted_iota(jnp.int32, (16, BLOCK), 0)
    for r in range(16):
        tile = coeff_ref[r, BLOCK:, pl.ds(pl.multiple_of(y * BLOCK, BLOCK), BLOCK)].astype(F32)
        for which in range(2):
            chosen = lax.rem(packed_row, 8) == x + 4 * which
            line = jnp.sum(jnp.where(chosen, tile, 0.0), axis=0, keepdims=True)
            rates[which, r // 2 : r // 2 + 1, r % 2 * BLOCK : (r % 2 + 1) * BLOCK] = line
    dt = rates[0]
    run = dot(rates[1], upper.astype(F32), precision=HIGH)
    closing = run[:, CHUNK - 1 :]
    from_start = jnp.exp(run)
    to_end = jnp.exp(closing - run)
    through = jnp.exp(closing)
    run_t = run.T

    for k in range(DEPTH):
        at = lanes(k)
        span = pl.ds(k * CHUNK, CHUNK)
        pre = ordered(summed(0, 0, at), summed(1, 0, at))
        grad = ordered(summed(0, 1, at), summed(1, 1, at)).astype(BF16)
        pre_s[:, span] = pre
        signal = (pre / (1.0 + jnp.exp(-pre))).astype(BF16)
        x_s[0, :, span] = signal
        x_s[1, :, span] = grad
        carried = (signal.astype(F32) * (dt[k : k + 1] * to_end[k : k + 1])).astype(BF16)
        states[k + 1] = dot(carried, coeffs(k, 0))
        arrived = (grad.astype(F32) * from_start[k : k + 1]).astype(BF16)
        cots[k] = dot(arrived, coeffs(k, 1))
    states[0] = start_ref[...]
    cots[DEPTH] = final_ref[...]
    for k in range(DEPTH):
        states[k + 1] = states[k + 1] + through[k : k + 1] * states[k]
    for k in reversed(range(DEPTH)):
        cots[k] = cots[k] + through[k : k + 1] * cots[k + 1]

    last = lax.broadcasted_iota(jnp.int32, (1, CHUNK), 1) == CHUNK - 1
    for k in range(DEPTH):
        at = lanes(k)
        span = pl.ds(k * CHUNK, CHUNK)
        signal, grad, pre = x_s[0, :, span], x_s[1, :, span], pre_s[:, span]
        b, c = coeffs(k, 0), coeffs(k, 1)
        step = dt[k : k + 1]
        rise, fall = from_start[k : k + 1], to_end[k : k + 1]
        signal32, grad32 = signal.astype(F32), grad.astype(F32)
        stepped32 = signal32 * step
        stepped = stepped32.astype(BF16)
        carried = (stepped32 * fall).astype(BF16)
        arrived = (grad32 * rise).astype(BF16)
        state, cot = states[k].astype(BF16), cots[k + 1].astype(BF16)
        decay = jnp.where(
            upper, jnp.exp(jnp.minimum(run[k : k + 1] - run_t[:, k : k + 1], 0.0)), 0.0
        )
        mixing = (dot(b, c, NT) * decay).astype(BF16)
        out = dot(stepped, mixing) + dot(state, c, NT) * rise
        back = dot(grad, mixing, NT) + dot(cot, b, NT) * fall
        pair = (dot(stepped, grad, TN) * decay).astype(BF16)
        b_grad = dot(pair, c) + dot(carried, cot, TN)
        c_grad = dot(pair, b, TN) + dot(arrived, state, TN)
        sig = 1.0 / (1.0 + jnp.exp(-pre))
        pre_grad = (back * step) * (sig * (1.0 + pre * (1.0 - sig)))
        for which, value in enumerate((pre_grad, out)):
            left, right = value[:, :BLOCK], value[:, BLOCK:]
            own_mine[which, :, at] = jnp.where(even, left, right).astype(BF16)
            own_theirs[which, :, at] = jnp.where(even, right, left).astype(BF16)
        low = jnp.concatenate([b_grad[:, :BLOCK], c_grad[:, :BLOCK]], axis=1)
        high = jnp.concatenate([b_grad[:, BLOCK:], c_grad[:, BLOCK:]], axis=1)
        for h in range(2):
            rows_h = slice(h * BLOCK, (h + 1) * BLOCK)
            mine_ref[2 * k + h, :BLOCK, :] = jnp.where(even, low[rows_h], high[rows_h]).astype(BF16)
            theirs_ref[2 * k + h, :BLOCK, :] = jnp.where(
                even, high[rows_h], low[rows_h]
            ).astype(BF16)
        step_grad = jnp.sum(signal32 * back, axis=0, keepdims=True)
        steps[k : k + 1, :] = step_grad
        anchor = jnp.sum(states[k + 1] * cots[k + 1])
        turned = jnp.sum(grad32 * out, axis=0, keepdims=True) - step * step_grad
        weigh[k : k + 1, :] = turned + jnp.where(last, anchor, 0.0)
    decays = dot(weigh[...], (rows >= cols).astype(F32), precision=HIGH)
    blank = jnp.zeros((16, STATE), F32)
    which_row = lax.broadcasted_iota(jnp.int32, (16, STATE), 0)
    for k in range(DEPTH):
        for h in range(2):
            span = slice(h * BLOCK, (h + 1) * BLOCK)
            line = jnp.concatenate([steps[k : k + 1, span], decays[k : k + 1, span]], axis=1)
            coarse = line.astype(BF16).astype(F32)
            tile = jnp.where(which_row == 0, coarse, jnp.where(which_row == 1, line - coarse, 0.0))
            mine_ref[2 * k + h, BLOCK:, :] = tile.astype(BF16)
            theirs_ref[2 * k + h, BLOCK:, :] = blank.astype(BF16)


def run_scan(place, sums, coeffs, start, final):
    tokens = DEPTH * CHUNK
    half = jax.ShapeDtypeStruct((2, HEAD_DIM, tokens // 2), BF16)
    grads = jax.ShapeDtypeStruct((16, BLOCK + 16, STATE), BF16)
    return pl.pallas_call(
        scan_kernel,
        out_shape=[half, half, grads, grads],
        in_specs=[SM] + [VM] * 9,
        out_specs=[VM] * 4,
        scratch_shapes=[
            pltpu.VMEM((2, HEAD_DIM, tokens), BF16),
            pltpu.VMEM((HEAD_DIM, tokens), F32),
            pltpu.VMEM((DEPTH + 1, HEAD_DIM, STATE), F32),
            pltpu.VMEM((DEPTH + 1, HEAD_DIM, STATE), F32),
            pltpu.VMEM((DEPTH, CHUNK), F32),
            pltpu.VMEM((DEPTH, CHUNK), F32),
            pltpu.VMEM((2, DEPTH, CHUNK), F32),
        ],
        compiler_params=ROOM,
        cost_estimate=pl.CostEstimate(
            flops=2_000_000_000, bytes_accessed=10_000_000, transcendentals=1_000_000
        ),
    )(place, *sums, coeffs, start, final)


def body(
    layer_input,
    output_grad,
    inproj_weight,
    outproj_weight,
    input_coeffs,
    output_coeffs,
    step_sizes,
    log_decay,
    state_start,
    state_grad,
):
    row = lax.axis_index("row")
    column = lax.axis_index("col")
    x, y = row // SIDE, row % SIDE
    z, core = column // 2, column % 2
    place = jnp.stack([z, core, x, y]).astype(jnp.int32)
    group = z * STATE
    rates = jnp.concatenate([step_sizes, log_decay], axis=0).reshape(8, 2 * STATE)
    coarse = lax.reduce_precision(rates, 8, 7)
    coeffs = jnp.concatenate(
        [
            jnp.concatenate(
                [
                    lax.dynamic_slice_in_dim(input_coeffs, group, STATE, 1),
                    lax.dynamic_slice_in_dim(output_coeffs, group, STATE, 1),
                ],
                axis=1,
            ),
            coarse.astype(BF16),
            (rates - coarse).astype(BF16),
        ],
        axis=0,
    )
    own_coeffs = coeffs
    coeffs = lax.all_gather(coeffs, "row", axis=0, tiled=True).reshape(16, BLOCK + 16, 2 * STATE)
    start = lax.dynamic_index_in_dim(state_start, row, 0, False)
    final = lax.dynamic_index_in_dim(state_grad, row, 0, False)
    in_w = inproj_weight.T

    packed_mine = pack(gather_z(layer_input), gather_z(output_grad), own_coeffs)
    packed_theirs = swap_core(packed_mine)
    units = [
        project(place, packed_mine, in_w, outproj_weight, True),
        project(place, packed_theirs, in_w, outproj_weight, False),
    ]
    units = reduce_pair(units, (shift_y, shift_x), coeffs)
    sums_mine, sums_theirs = reduce_small(units, (shift_x, shift_y))

    own_mine, own_theirs, mine, theirs = run_scan(
        place, [*sums_mine, *sums_theirs], coeffs, start, final
    )
    pieces_mine, pieces_theirs = gather_small((own_mine, own_theirs), (shift_y, shift_x))
    units = (
        line_up(place, pieces_mine, 3, *pieces_theirs[2:4]),
        line_up(place, pieces_theirs, 2, *pieces_mine[2:4]),
    )
    pieces_mine, pieces_theirs = gather_pair(units, (shift_x, shift_y))
    both = bump(mine, swap_core(theirs), 0, pieces_mine[6])
    both = lax.all_to_all(both, "row", 0, 0)
    pg_theirs, so_theirs, update_theirs = run_update(place, pieces_theirs, in_w, False)
    pg_mine, so_mine, update_mine = run_update(place, pieces_mine, in_w, True, update_theirs)
    update_theirs = swap_core(update_theirs)
    input_grad, first, second = scatter_z(add(update_mine, update_theirs).astype(BF16), both)
    inproj_grad = weight_grad(pg_mine, packed_mine, pg_theirs, packed_theirs, 0, first)
    outproj_grad = weight_grad(so_mine, packed_mine, so_theirs, packed_theirs, 1, second)

    coeff_grads = jnp.sum(both[:, :BLOCK].astype(F32), axis=0)
    lines = add(both[:, BLOCK], both[:, BLOCK + 1])
    return (
        input_grad,
        inproj_grad,
        outproj_grad,
        coeff_grads[:, :BLOCK],
        coeff_grads[:, BLOCK:],
        lines[:, :BLOCK],
        lines[:, BLOCK:],
    )


def solution(mesh):
    return jax.shard_map(
        body,
        mesh=mesh,
        in_specs=(
            P("col", "row"),
            P("col", "row"),
            P("row", "col"),
            P("col", "row"),
            P("row", None),
            P("row", None),
            P("col", "row"),
            P("col", "row"),
            P("col", None, None),
            P("col", None, None),
        ),
        out_specs=(
            P("col", "row"),
            P("row", "col"),
            P("col", "row"),
            P("row", "col"),
            P("row", "col"),
            P("col", "row"),
            P("col", "row"),
        ),
        check_vma=False,
    )
```

```python
import functools

import jax
import jax.numpy as jnp
from jax import lax
from jax.experimental import pallas as pl
from jax.experimental.pallas import tpu as pltpu
from jax.sharding import PartitionSpec as P

HEAD_DIM = 64
STATE = 256
SIDE = 4
DEPTH = 8
BLOCK = 128
CHUNK = 256
F32 = jnp.float32
BF16 = jnp.bfloat16
VM = pl.BlockSpec(memory_space=pltpu.VMEM)
SM = pl.BlockSpec(memory_space=pltpu.SMEM)
ANY = pl.BlockSpec(memory_space=pl.ANY)
ROOM = pltpu.CompilerParams(vmem_limit_bytes=40 * 1024 * 1024)
SMALL = pltpu.CompilerParams(vmem_limit_bytes=6 * 1024 * 1024)


def shift_y(a, d):
    pairs = [(x * 4 + y, x * 4 + (y + d) % 4) for x in range(4) for y in range(4)]
    return lax.ppermute(a, "row", pairs)


def shift_x(a, d):
    pairs = [(x * 4 + y, (x + d) % 4 * 4 + y) for x in range(4) for y in range(4)]
    return lax.ppermute(a, "row", pairs)


def shift_z(a, d):
    pairs = [(z * 2 + c, (z + d) % 8 * 2 + c) for z in range(8) for c in range(2)]
    return lax.ppermute(a, "col", pairs)


def swap_core(a):
    return lax.ppermute(a, "col", [(i, i ^ 1) for i in range(16)])


def add(*terms):
    total = terms[0].astype(F32)
    for term in terms[1:]:
        total = total + term.astype(F32)
    return total


def gather_z(own):
    half = own.shape[0] // 2
    up1, down1 = shift_z(own, 1), shift_z(own, -1)
    up2, down2 = shift_z(up1, 1), shift_z(down1, -1)
    up3, down3 = shift_z(up2, 1), shift_z(down2, -1)
    far = (shift_z(up3[:half], 1), shift_z(down3[half:], -1))
    return [own, down1, down2, down3, *far, up3, up2, up1]


def bump_kernel(first, base, extra, *refs):
    out = refs[-1]
    if extra.shape == base.shape:
        out[...] = add(base[...], extra[...]).astype(BF16)
    else:
        out[...] = base[...]
        at = pl.ds(first, extra.shape[0])
        out[at] = add(base[at], extra[...]).astype(BF16)


def bump(base, extra, first, *waits):
    return pl.pallas_call(
        functools.partial(bump_kernel, first),
        out_shape=jax.ShapeDtypeStruct(base.shape, BF16),
        in_specs=[VM, VM] + [ANY] * len(waits),
        out_specs=VM,
        compiler_params=SMALL,
    )(base, extra, *waits)


def own_kernel(c0, first_up, second_up, first_down, second_down, *refs):
    outs = refs[-5:]
    half = first_up.shape[0]
    near = add(c0[:half], first_up[...], first_down[...]).astype(BF16)
    away = add(c0[half:], second_up[...], second_down[...]).astype(BF16)
    outs[0][...] = near[0]
    outs[1][...] = near[1]
    outs[2][...] = away[0, :1]
    outs[3][...] = away[0, 1:]
    outs[4][...] = away[1]


def own_sum(c0, pieces, *waits):
    whole = jax.ShapeDtypeStruct(c0.shape[1:], BF16)
    half = jax.ShapeDtypeStruct((1, *c0.shape[2:]), BF16)
    return pl.pallas_call(
        own_kernel,
        out_shape=[whole, whole, half, half, whole],
        in_specs=[VM] * 5 + [ANY] * len(waits),
        out_specs=[VM] * 5,
        compiler_params=SMALL,
    )(c0, *pieces, *waits)


def reduce_pair(units, shifts, *waits):
    far, free = [], []
    for (c0, c1a, c1b, c2a, c2b, c3a, c3b), shift in zip(units, shifts):
        far.append((shift(c2a, 1), shift(c2b, -1)))
        free.append((shift(c1b, 1), shift(c3a, -1)))
    sums = []
    for i, shift in enumerate(shifts):
        c0, c1a, c1b, c2a, c2b, c3a, c3b = units[i]
        other = far[1 - i]
        last_up = shift(bump(c1a, far[i][0], 0, *other), 1)
        last_down = shift(bump(c3b, far[i][1], 0, *other), -1)
        sums.append((c0, (last_up, free[i][0], free[i][1], last_down)))
    return [own_sum(c0, pieces, *waits) for c0, pieces in sums]


def reduce_small(units, shifts):
    far = [
        (shift(c2a, 1), shift(c2b, -1))
        for (c0, c1, c2a, c2b, c3), shift in zip(units, shifts)
    ]
    parts = []
    for i, shift in enumerate(shifts):
        c0, c1, c2a, c2b, c3 = units[i]
        other = far[1 - i]
        up = shift(bump(c1, far[i][0], 0, *other), 1)
        down = shift(bump(c3, far[i][1], 1, *other), -1)
        parts.append((c0, up, down))
    return parts


def cut_kernel(first, base, *refs):
    out = refs[-1]
    out[...] = base[pl.ds(first, out.shape[0])]


def cut(base, first, *waits):
    half = base.shape[0] // 2
    return pl.pallas_call(
        functools.partial(cut_kernel, first * half),
        out_shape=jax.ShapeDtypeStruct((half, *base.shape[1:]), BF16),
        in_specs=[VM] + [ANY] * len(waits),
        out_specs=VM,
        compiler_params=SMALL,
    )(base, *waits)


def gather_small(units, shifts):
    near = [(shift(own, 1), shift(own, -1)) for own, shift in zip(units, shifts)]
    lines = []
    for i, shift in enumerate(shifts):
        (up, down), other = near[i], near[1 - i]
        far = shift(cut(up, 0, *other), 1), shift(cut(down, 1, *other), -1)
        lines.append((units[i], down, *far, up))
    return lines


def gather_pair(units, shifts):
    first = [(shift(lo, 1), shift(hi, -1)) for (lo, hi), shift in zip(units, shifts)]
    rest = [(shift(hi, 1), shift(lo, -1)) for (lo, hi), shift in zip(units, shifts)]
    far = [(shift(up, 1), shift(down, -1)) for (up, down), shift in zip(first, shifts)]
    return [
        (lo, hi, down_lo, down_hi, far_lo, far_hi, up_lo, up_hi)
        for (lo, hi), (up_lo, down_hi), (up_hi, down_lo), (far_lo, far_hi) in zip(
            units, first, rest, far
        )
    ]


def scatter_z(total, *waits):
    rows = total.shape[0] // DEPTH
    half = rows // 2
    chunks = [total[d * rows : (d + 1) * rows] for d in range(DEPTH)]
    up = shift_z(chunks[4][:half], 1)
    down = shift_z(chunks[4][half:], -1)
    up = first = bump(chunks[3], up, 0)
    up, down = shift_z(up, 1), shift_z(bump(chunks[5], down, half), -1)
    up = second = bump(chunks[2], up, 0)
    up, down = shift_z(up, 1), shift_z(bump(chunks[6], down, 0), -1)
    up = shift_z(bump(chunks[1], up, 0, *waits), 1)
    down = shift_z(bump(chunks[7], down, 0), -1)
    return add(chunks[0], up, down).astype(BF16), first, second


def dot(a, b, dims=((1,), (0,)), precision=None):
    return lax.dot_general(a, b, (dims, ((), ())), preferred_element_type=F32, precision=precision)


NT = ((1,), (1,))
TN = ((0,), (0,))
HIGH = lax.Precision.HIGHEST


def turn(at, d):
    return lax.rem(at + d, SIDE)


def pack_kernel(*refs):
    out = refs[-1]
    pieces = refs[:18]
    for which in range(2):
        row = 0
        for piece in pieces[which * 9 : which * 9 + 9]:
            out[which, row : row + piece.shape[0], :] = piece[...]
            row += piece.shape[0]


def pack(inputs, grads, *waits):
    shape = (2, DEPTH * BLOCK, inputs[0].shape[1])
    return pl.pallas_call(
        pack_kernel,
        out_shape=jax.ShapeDtypeStruct(shape, BF16),
        in_specs=[VM] * 18 + [ANY] * len(waits),
        out_specs=VM,
        compiler_params=ROOM,
    )(*inputs, *grads, *waits)


def project_kernel(y_first, place, tokens_ref, in_w, grad_w, c0, c1a, c1b, c2a, c2b, c3a, c3b):
    x, y = place[2], place[3]
    halves = ((c0, c0), (c1a, c1b), (c2a, c2b), (c3a, c3b))

    def one(tile, carry):
        span = pl.ds(pl.multiple_of(tile * CHUNK, CHUNK), CHUNK)
        for which, w_ref in enumerate((in_w, grad_w)):
            tokens = tokens_ref[which, span, :]
            for d in range(SIDE):
                pieces = []
                for i in range(SIDE):
                    at_x, at_y = (turn(x, i), turn(y, d)) if y_first else (turn(x, d), turn(y, i))
                    start = pl.multiple_of((at_x * SIDE + at_y) * HEAD_DIM, HEAD_DIM)
                    pieces.append(w_ref[pl.ds(start, HEAD_DIM), :])
                part = dot(jnp.concatenate(pieces, axis=0), tokens, NT).astype(BF16)
                for i in range(SIDE):
                    rows = part[i * HEAD_DIM : (i + 1) * HEAD_DIM]
                    halves[d][i // 2][i if d == 0 else i % 2, which, :, span] = rows
        return carry

    lax.fori_loop(0, DEPTH * BLOCK // CHUNK, one, 0)


def project(place, tokens, in_w, grad_w, y_first):
    count, width = tokens.shape[1:]
    chunk = jax.ShapeDtypeStruct((SIDE, 2, HEAD_DIM, count), BF16)
    half = jax.ShapeDtypeStruct((SIDE // 2, 2, HEAD_DIM, count), BF16)
    return pl.pallas_call(
        functools.partial(project_kernel, y_first),
        out_shape=[chunk] + [half] * 6,
        in_specs=[SM] + [VM] * 3,
        out_specs=[VM] * 7,
        compiler_params=ROOM,
        cost_estimate=pl.CostEstimate(
            flops=4 * 1024 * count * width, bytes_accessed=10_000_000, transcendentals=0
        ),
    )(place, tokens, in_w, grad_w)


def line_kernel(axis, place, own, down, far_a, far_b, up, *refs):
    outs = refs[-2:]
    at = place[axis]
    for slot in range(SIDE):
        d = lax.rem(slot - at + SIDE, SIDE)
        target = outs[slot // 2].at[slot % 2]
        far = jnp.concatenate([far_a[...], far_b[...]], axis=0)
        near = jnp.where(d == 0, own[...], down[...])
        away = jnp.where(d == 2, far, up[...])
        target[...] = jnp.where(d < 2, near, away)


def line_up(place, pieces, axis, *waits):
    half = jax.ShapeDtypeStruct((SIDE // 2, *pieces[0].shape), BF16)
    return pl.pallas_call(
        functools.partial(line_kernel, axis),
        out_shape=[half, half],
        in_specs=[SM] + [VM] * 5 + [ANY] * len(waits),
        out_specs=[VM] * 2,
        compiler_params=SMALL,
    )(place, *pieces, *waits)


def update_kernel(y_first, place, *refs):
    x, y = place[2], place[3]
    w_ref, (grads, outs, update) = refs[8], refs[-3:]
    for n, ref in enumerate(refs[:8]):
        d = n // 2
        for i in range(2):
            slot = n % 2 * 2 + i
            at_x, at_y = (turn(x, d), slot) if y_first else (slot, turn(y, d))
            start = pl.multiple_of((at_x * SIDE + at_y) * HEAD_DIM, HEAD_DIM)
            grads[pl.ds(start, HEAD_DIM), :] = ref[i, 0]
            outs[pl.ds(start, HEAD_DIM), :] = ref[i, 1]
    for tile in range(DEPTH * BLOCK // CHUNK):
        span = pl.ds(tile * CHUNK, CHUNK)
        update[span, :] = dot(grads[:, span], w_ref[...], TN).astype(BF16)


def run_update(place, pieces, w, y_first, *waits):
    tokens = pieces[0].shape[-1]
    whole = jax.ShapeDtypeStruct((w.shape[0], tokens), BF16)
    return pl.pallas_call(
        functools.partial(update_kernel, y_first),
        out_shape=[whole, whole, jax.ShapeDtypeStruct((tokens, w.shape[1]), BF16)],
        in_specs=[SM] + [VM] * 9 + [ANY] * len(waits),
        out_specs=[VM] * 3,
        compiler_params=ROOM,
        cost_estimate=pl.CostEstimate(
            flops=2 * w.size * tokens, bytes_accessed=6_000_000, transcendentals=0
        ),
    )(place, *pieces, w, *waits)


def weight_kernel(which, a_mine, b_mine, a_theirs, b_theirs, *refs):
    out = refs[-1]
    for tile in range(a_mine.shape[0] // CHUNK):
        span = pl.ds(tile * CHUNK, CHUNK)
        part = dot(a_mine[span, :], b_mine[which]) + dot(a_theirs[span, :], b_theirs[which])
        if which == 0:
            out[:, span] = part.T
        else:
            out[span, :] = part


def weight_grad(a_mine, b_mine, a_theirs, b_theirs, which, *waits):
    rows, cols = a_mine.shape[0], b_mine.shape[2]
    return pl.pallas_call(
        functools.partial(weight_kernel, which),
        out_shape=jax.ShapeDtypeStruct((rows, cols) if which else (cols, rows), F32),
        in_specs=[VM] * 4 + [ANY] * len(waits),
        out_specs=VM,
        compiler_params=ROOM,
        cost_estimate=pl.CostEstimate(
            flops=4 * rows * cols * a_mine.shape[1], bytes_accessed=8_000_000, transcendentals=0
        ),
    )(a_mine, b_mine, a_theirs, b_theirs, *waits)


def scan_kernel(place, *refs):
    sums = refs[:6]
    coeff_ref, start_ref, final_ref = refs[6:9]
    own_mine, own_theirs, mine_ref, theirs_ref = refs[9:13]
    x_s, pre_s, states, cots, weigh, steps, rates = refs[13:]
    z, core = place[0], place[1]
    even = core == 0

    def lanes(k):
        return pl.ds(pl.multiple_of(lax.rem(k - z + DEPTH, DEPTH) * BLOCK, BLOCK), BLOCK)

    def summed(unit, which, at):
        return add(*(ref[which, :, at] for ref in sums[unit * 3 : unit * 3 + 3]))

    def ordered(mine, theirs):
        return jnp.concatenate(
            [jnp.where(even, mine, theirs), jnp.where(even, theirs, mine)], axis=1
        )

    def coeffs(k, which):
        block = coeff_ref[2 * k : 2 * k + 2, :BLOCK, which * STATE : (which + 1) * STATE]
        return block.reshape(CHUNK, STATE)

    rows = lax.broadcasted_iota(jnp.int32, (CHUNK, CHUNK), 0)
    cols = lax.broadcasted_iota(jnp.int32, (CHUNK, CHUNK), 1)
    upper = rows <= cols
    x, y = place[2], place[3]
    packed_row = lax.broadcasted_iota(jnp.int32, (16, BLOCK), 0)
    for r in range(16):
        tile = coeff_ref[r, BLOCK:, pl.ds(pl.multiple_of(y * BLOCK, BLOCK), BLOCK)].astype(F32)
        for which in range(2):
            chosen = lax.rem(packed_row, 8) == x + 4 * which
            line = jnp.sum(jnp.where(chosen, tile, 0.0), axis=0, keepdims=True)
            rates[which, r // 2 : r // 2 + 1, r % 2 * BLOCK : (r % 2 + 1) * BLOCK] = line
    dt = rates[0]
    run = dot(rates[1], upper.astype(F32), precision=HIGH)
    closing = run[:, CHUNK - 1 :]
    from_start = jnp.exp(run)
    to_end = jnp.exp(closing - run)
    through = jnp.exp(closing)
    run_t = run.T

    for k in range(DEPTH):
        at = lanes(k)
        span = pl.ds(k * CHUNK, CHUNK)
        pre = ordered(summed(0, 0, at), summed(1, 0, at))
        grad = ordered(summed(0, 1, at), summed(1, 1, at)).astype(BF16)
        pre_s[:, span] = pre
        signal = (pre / (1.0 + jnp.exp(-pre))).astype(BF16)
        x_s[0, :, span] = signal
        x_s[1, :, span] = grad
        carried = (signal.astype(F32) * (dt[k : k + 1] * to_end[k : k + 1])).astype(BF16)
        states[k + 1] = dot(carried, coeffs(k, 0))
        arrived = (grad.astype(F32) * from_start[k : k + 1]).astype(BF16)
        cots[k] = dot(arrived, coeffs(k, 1))
    states[0] = start_ref[...]
    cots[DEPTH] = final_ref[...]
    for k in range(DEPTH):
        states[k + 1] = states[k + 1] + through[k : k + 1] * states[k]
    for k in reversed(range(DEPTH)):
        cots[k] = cots[k] + through[k : k + 1] * cots[k + 1]

    last = lax.broadcasted_iota(jnp.int32, (1, CHUNK), 1) == CHUNK - 1
    for k in range(DEPTH):
        at = lanes(k)
        span = pl.ds(k * CHUNK, CHUNK)
        signal, grad, pre = x_s[0, :, span], x_s[1, :, span], pre_s[:, span]
        b, c = coeffs(k, 0), coeffs(k, 1)
        step = dt[k : k + 1]
        rise, fall = from_start[k : k + 1], to_end[k : k + 1]
        signal32, grad32 = signal.astype(F32), grad.astype(F32)
        stepped32 = signal32 * step
        stepped = stepped32.astype(BF16)
        carried = (stepped32 * fall).astype(BF16)
        arrived = (grad32 * rise).astype(BF16)
        state, cot = states[k].astype(BF16), cots[k + 1].astype(BF16)
        decay = jnp.where(
            upper, jnp.exp(jnp.minimum(run[k : k + 1] - run_t[:, k : k + 1], 0.0)), 0.0
        )
        mixing = (dot(b, c, NT) * decay).astype(BF16)
        out = dot(stepped, mixing) + dot(state, c, NT) * rise
        back = dot(grad, mixing, NT) + dot(cot, b, NT) * fall
        pair = (dot(stepped, grad, TN) * decay).astype(BF16)
        b_grad = dot(pair, c) + dot(carried, cot, TN)
        c_grad = dot(pair, b, TN) + dot(arrived, state, TN)
        sig = 1.0 / (1.0 + jnp.exp(-pre))
        pre_grad = (back * step) * (sig * (1.0 + pre * (1.0 - sig)))
        for which, value in enumerate((pre_grad, out)):
            left, right = value[:, :BLOCK], value[:, BLOCK:]
            own_mine[which, :, at] = jnp.where(even, left, right).astype(BF16)
            own_theirs[which, :, at] = jnp.where(even, right, left).astype(BF16)
        low = jnp.concatenate([b_grad[:, :BLOCK], c_grad[:, :BLOCK]], axis=1)
        high = jnp.concatenate([b_grad[:, BLOCK:], c_grad[:, BLOCK:]], axis=1)
        for h in range(2):
            rows_h = slice(h * BLOCK, (h + 1) * BLOCK)
            mine_ref[2 * k + h, :BLOCK, :] = jnp.where(even, low[rows_h], high[rows_h]).astype(BF16)
            theirs_ref[2 * k + h, :BLOCK, :] = jnp.where(
                even, high[rows_h], low[rows_h]
            ).astype(BF16)
        step_grad = jnp.sum(signal32 * back, axis=0, keepdims=True)
        steps[k : k + 1, :] = step_grad
        anchor = jnp.sum(states[k + 1] * cots[k + 1])
        turned = jnp.sum(grad32 * out, axis=0, keepdims=True) - step * step_grad
        weigh[k : k + 1, :] = turned + jnp.where(last, anchor, 0.0)
    decays = dot(weigh[...], (rows >= cols).astype(F32), precision=HIGH)
    blank = jnp.zeros((16, STATE), F32)
    which_row = lax.broadcasted_iota(jnp.int32, (16, STATE), 0)
    for k in range(DEPTH):
        for h in range(2):
            span = slice(h * BLOCK, (h + 1) * BLOCK)
            line = jnp.concatenate([steps[k : k + 1, span], decays[k : k + 1, span]], axis=1)
            coarse = line.astype(BF16).astype(F32)
            tile = jnp.where(which_row == 0, coarse, jnp.where(which_row == 1, line - coarse, 0.0))
            mine_ref[2 * k + h, BLOCK:, :] = tile.astype(BF16)
            theirs_ref[2 * k + h, BLOCK:, :] = blank.astype(BF16)


def run_scan(place, sums, coeffs, start, final):
    tokens = DEPTH * CHUNK
    half = jax.ShapeDtypeStruct((2, HEAD_DIM, tokens // 2), BF16)
    grads = jax.ShapeDtypeStruct((16, BLOCK + 16, STATE), BF16)
    return pl.pallas_call(
        scan_kernel,
        out_shape=[half, half, grads, grads],
        in_specs=[SM] + [VM] * 9,
        out_specs=[VM] * 4,
        scratch_shapes=[
            pltpu.VMEM((2, HEAD_DIM, tokens), BF16),
            pltpu.VMEM((HEAD_DIM, tokens), F32),
            pltpu.VMEM((DEPTH + 1, HEAD_DIM, STATE), F32),
            pltpu.VMEM((DEPTH + 1, HEAD_DIM, STATE), F32),
            pltpu.VMEM((DEPTH, CHUNK), F32),
            pltpu.VMEM((DEPTH, CHUNK), F32),
            pltpu.VMEM((2, DEPTH, CHUNK), F32),
        ],
        compiler_params=ROOM,
        cost_estimate=pl.CostEstimate(
            flops=2_000_000_000, bytes_accessed=10_000_000, transcendentals=1_000_000
        ),
    )(place, *sums, coeffs, start, final)


def body(
    layer_input,
    output_grad,
    inproj_weight,
    outproj_weight,
    input_coeffs,
    output_coeffs,
    step_sizes,
    log_decay,
    state_start,
    state_grad,
):
    row = lax.axis_index("row")
    column = lax.axis_index("col")
    x, y = row // SIDE, row % SIDE
    z, core = column // 2, column % 2
    place = jnp.stack([z, core, x, y]).astype(jnp.int32)
    group = z * STATE
    rates = jnp.concatenate([step_sizes, log_decay], axis=0).reshape(8, 2 * STATE)
    coarse = lax.reduce_precision(rates, 8, 7)
    coeffs = jnp.concatenate(
        [
            jnp.concatenate(
                [
                    lax.dynamic_slice_in_dim(input_coeffs, group, STATE, 1),
                    lax.dynamic_slice_in_dim(output_coeffs, group, STATE, 1),
                ],
                axis=1,
            ),
            coarse.astype(BF16),
            (rates - coarse).astype(BF16),
        ],
        axis=0,
    )
    own_coeffs = coeffs
    coeffs = lax.all_gather(coeffs, "row", axis=0, tiled=True).reshape(16, BLOCK + 16, 2 * STATE)
    start = lax.dynamic_index_in_dim(state_start, row, 0, False)
    final = lax.dynamic_index_in_dim(state_grad, row, 0, False)
    in_w = inproj_weight.T

    packed_mine = pack(gather_z(layer_input), gather_z(output_grad), own_coeffs)
    packed_theirs = swap_core(packed_mine)
    units = [
        project(place, packed_mine, in_w, outproj_weight, True),
        project(place, packed_theirs, in_w, outproj_weight, False),
    ]
    units = reduce_pair(units, (shift_y, shift_x), coeffs)
    sums_mine, sums_theirs = reduce_small(units, (shift_x, shift_y))

    own_mine, own_theirs, mine, theirs = run_scan(
        place, [*sums_mine, *sums_theirs], coeffs, start, final
    )
    pieces_mine, pieces_theirs = gather_small((own_mine, own_theirs), (shift_y, shift_x))
    swapped = swap_core(theirs)
    units = (
        line_up(place, pieces_mine, 3, *pieces_theirs[2:4], swapped),
        line_up(place, pieces_theirs, 2, *pieces_mine[2:4], swapped),
    )
    pieces_mine, pieces_theirs = gather_pair(units, (shift_x, shift_y))
    pg_theirs, so_theirs, update_theirs = run_update(
        place, pieces_theirs, in_w, False, *(p for p in pieces_mine if p is not None)
    )
    pg_mine, so_mine, update_mine = run_update(place, pieces_mine, in_w, True, update_theirs)
    both = bump(mine, swapped, 0, update_mine)
    both = lax.all_to_all(both, "row", 0, 0)
    update_theirs = swap_core(update_theirs)
    input_grad, first, second = scatter_z(add(update_mine, update_theirs).astype(BF16), both)
    inproj_grad = weight_grad(pg_mine, packed_mine, pg_theirs, packed_theirs, 0, first)
    outproj_grad = weight_grad(so_mine, packed_mine, so_theirs, packed_theirs, 1, second)

    coeff_grads = jnp.sum(both[:, :BLOCK].astype(F32), axis=0)
    lines = add(both[:, BLOCK], both[:, BLOCK + 1])
    return (
        input_grad,
        inproj_grad,
        outproj_grad,
        coeff_grads[:, :BLOCK],
        coeff_grads[:, BLOCK:],
        lines[:, :BLOCK],
        lines[:, BLOCK:],
    )


def solution(mesh):
    return jax.shard_map(
        body,
        mesh=mesh,
        in_specs=(
            P("col", "row"),
            P("col", "row"),
            P("row", "col"),
            P("col", "row"),
            P("row", None),
            P("row", None),
            P("col", "row"),
            P("col", "row"),
            P("col", None, None),
            P("col", None, None),
        ),
        out_specs=(
            P("col", "row"),
            P("row", "col"),
            P("col", "row"),
            P("row", "col"),
            P("row", "col"),
            P("col", "row"),
            P("col", "row"),
        ),
        check_vma=False,
    )
```
